512 devices in a mesh: lon: 16 (over y, x_lo, core), lat: 32 (over z, x_hi).
Axes of the slice: x: 4 (x_hi: 2, x_lo: 2; x = x_hi * 2 + x_lo), y: 4, z: 16, core: 2. Of those that a mesh axis runs over, the one named last changes fastest.
Arguments:
- field: bfloat16 [256, 2048, 256], P('lat', 'lon'), may hold values from -6 to 6
- conv_weight: bfloat16 [3, 3, 256, 256], replicated, may hold values from -0.125 to 0.125
- query_weight: bfloat16 [256, 1024], replicated, may hold values from -3.6 to 3.6
- key_weight: bfloat16 [256, 1024], replicated, may hold values from -0.6 to 0.6
- value_weight: bfloat16 [256, 1024], replicated, may hold values from -0.375 to 0.375
- query_rows: int32 [32, 16, 1], P('lat', 'lon'), may hold values from 0 to 1, as said below
- attended_grad: bfloat16 [32, 512, 1024], P('lat', 'lon'), may hold values from -6 to 6
Outputs:
- attended: bfloat16 [32, 512, 1024], P('lat', 'lon')
- field_grad: bfloat16 [256, 2048, 256], P('lat', 'lon')
The draws below stay inside these ranges and needn't reach their ends.
Inputs may be any that keep to these rules, and one draw needn't show every extreme that they name: `query_rows`: within one block the 1 entries are distinct and increasing.
All inputs are finite; a program needn't handle non-finite values.
Results may differ from the reference program's by a relative error of at most 0.033.
Values may be sent and summed in bfloat16 or wider, within the bound.
A program may use at most 128 MiB of HBM per device.

```python
import jax
import jax.numpy as jnp
from jax import lax

C = 256
AW = 1024
HEAD_DIM = 64
NLAT = 256
NLON = 2048
PROWS = 2
PCOLS = 32
QSEL = 1
N_LON = 16
N_LAT = 32


def projection_base(key):
    return jnp.clip(jax.random.normal(key, (C, AW), jnp.float32), -4.0, 4.0)


def draw_key_weight(key, part):
    shared_base = projection_base(key)
    return (0.11 * shared_base).astype(jnp.bfloat16)


def draw_query_weight(key, part):
    key = jax.random.fold_in(key, 12)
    fresh_normal = jnp.clip(jax.random.normal(key, (C, AW), jnp.float32), -4.0, 4.0)
    return (0.11 * fresh_normal).astype(jnp.bfloat16)


def draw_query_rows(key, part):
    key = jax.random.fold_in(key, 13)
    scores = jax.random.randint(key, (N_LAT, N_LON, PROWS), 0, 1 << 20) * PROWS + jnp.arange(PROWS, dtype=jnp.int32)
    ranking = jnp.argsort(scores, axis=-1, stable=True)[..., :QSEL]
    return jnp.sort(ranking, axis=-1).astype(jnp.int32)


def block_levels(stream_key, dims, split, least, largest):
    def one(axis_at, blocks):
        draws = jax.random.uniform(jax.random.fold_in(jax.random.fold_in(stream_key, 6), axis_at), (blocks,), jnp.float32, least / len(split), largest / len(split))
        return jnp.repeat(jnp.exp(draws), dims[axis_at] // blocks).reshape((-1,) + (1,) * (len(dims) - axis_at - 1))

    loudness = one(*split[0])
    for cut in split[1:]:
        loudness = loudness * one(*cut)
    return loudness


def bell_draw(own_key, shape, width, reach, pieces=(), kind=jnp.bfloat16):
    values = width * jax.random.normal(own_key, shape, jnp.float32)
    if pieces:
        values = values * block_levels(own_key, shape, pieces, -0.22, 0.18)
    return jnp.clip(values, -reach, reach).astype(kind)


def setup_inputs(seed: int = 0) -> dict:
    keys = jax.random.split(jax.random.key(seed), 8)
    field = bell_draw(keys[0], (NLAT, NLON, C), 1.0, 6.0, ((0, 32), (1, 16)))
    conv_weight = bell_draw(keys[1], (3, 3, C, C), (9 * C) ** -0.5, 0.125)
    query_weight = draw_query_weight(jax.random.fold_in(keys[7], 71), 0)
    key_weight = draw_key_weight(jax.random.fold_in(keys[7], 71), 0)
    value_weight = bell_draw(keys[4], (C, AW), C ** -0.5, 0.375)
    query_rows = draw_query_rows(jax.random.fold_in(keys[7], 71), 0)
    attended_grad = bell_draw(keys[6], (N_LAT * QSEL, NLON // 4, AW), 1.0, 6.0, ((0, 32), (1, 16)))
    return {"field": field, "conv_weight": conv_weight, "query_weight": query_weight, "key_weight": key_weight, "value_weight": value_weight, "query_rows": query_rows, "attended_grad": attended_grad}


norm_eps = 1e-05

def rounded(values_in):
    return lax.optimization_barrier(values_in.astype(jnp.bfloat16)).astype(jnp.float32)

def conv_wrap(grid_in, kernel):
    padded = jnp.concatenate([grid_in[:, -1:], grid_in, grid_in[:, :1]], axis=1)
    padded = jnp.pad(padded, ((1, 1), (0, 0), (0, 0)))
    result = lax.conv_general_dilated(padded[None].astype(jnp.float32), kernel.astype(jnp.float32), (1, 1), 'VALID', dimension_numbers=('NHWC', 'HWIO', 'NHWC'), precision=lax.Precision.HIGHEST)
    return result[0]

def reference(field, conv_weight, query_weight, key_weight, value_weight, query_rows, attended_grad):
    head_count = AW // HEAD_DIM
    score_scale = HEAD_DIM ** (-0.5)
    conv_out = conv_wrap(field, conv_weight)
    activated = jax.nn.silu(conv_out)
    pooled = activated.reshape(NLAT // 4, 4, NLON // 4, 4, C).mean(axis=(1, 3))
    row_mean = pooled.mean(-1, keepdims=True)
    centred = pooled - row_mean
    inv_std = lax.rsqrt((centred * centred).mean(-1, keepdims=True) + norm_eps)
    standard = centred * inv_std
    normed = standard.astype(jnp.bfloat16)
    flat_normed = normed.reshape(-1, C)
    key_rows = jnp.dot(flat_normed, key_weight, preferred_element_type=jnp.float32).astype(jnp.bfloat16)
    value_rows = jnp.dot(flat_normed, value_weight, preferred_element_type=jnp.float32).astype(jnp.bfloat16)
    key_rows = key_rows.reshape(N_LAT, PROWS * (NLON // 4), AW)
    value_rows = value_rows.reshape(N_LAT, PROWS * (NLON // 4), AW)
    onehot = (query_rows[..., None] == jnp.arange(PROWS, dtype=jnp.int32)).astype(jnp.float32)
    normed_five = normed.reshape(N_LAT, PROWS, N_LON, PCOLS, C).astype(jnp.float32)
    selected = jnp.einsum('blqr,brlsc->bqlsc', onehot, normed_five).astype(jnp.bfloat16)
    queries = jnp.dot(selected.reshape(-1, C), query_weight, preferred_element_type=jnp.float32).astype(jnp.bfloat16)
    queries = queries.reshape(N_LAT, QSEL, N_LON, PCOLS, AW)
    out_grads = attended_grad.reshape(N_LAT, QSEL, N_LON, PCOLS, AW)
    query_w32 = query_weight.astype(jnp.float32)
    key_w32 = key_weight.astype(jnp.float32)
    value_w32 = value_weight.astype(jnp.float32)

    def band_attention(inputs):
        band_keys, band_values, band_queries, band_grads, band_onehot = inputs
        key_total = band_keys.shape[0]
        query_heads = band_queries.reshape(-1, head_count, HEAD_DIM).astype(jnp.float32)
        key_heads = band_keys.reshape(key_total, head_count, HEAD_DIM).astype(jnp.float32)
        value_heads = band_values.reshape(key_total, head_count, HEAD_DIM).astype(jnp.float32)
        scores = jnp.einsum('qhd,khd->hqk', query_heads, key_heads) * score_scale
        row_max = scores.max(-1, keepdims=True)
        expo_terms = jnp.exp(scores - row_max)
        attn_probs = expo_terms / expo_terms.sum(-1, keepdims=True)
        probs_low = rounded(attn_probs)
        attn_out = jnp.einsum('hqk,khd->qhd', probs_low, value_heads)
        attended_band = attn_out.astype(jnp.bfloat16).reshape(QSEL, N_LON * PCOLS, AW)
        grad_heads = band_grads.reshape(-1, head_count, HEAD_DIM).astype(jnp.float32)
        dprob = jnp.einsum('qhd,khd->hqk', grad_heads, value_heads)
        row_delta = jnp.einsum('qhd,qhd->hq', grad_heads, attn_out)
        score_grad = rounded(attn_probs * (dprob - row_delta[:, :, None]) * score_scale)
        query_grad = rounded(jnp.einsum('hqk,khd->qhd', score_grad, key_heads)).reshape(-1, AW)
        query_feat = jnp.dot(query_grad, query_w32.T, precision=lax.Precision.HIGHEST).reshape(QSEL, N_LON, PCOLS, C)
        grad_five = score_grad.reshape(head_count, QSEL, N_LON, PCOLS, key_total)
        probs_five = probs_low.reshape(head_count, QSEL, N_LON, PCOLS, key_total)
        query_five = query_heads.reshape(QSEL, N_LON, PCOLS, head_count, HEAD_DIM)
        cotan_five = grad_heads.reshape(QSEL, N_LON, PCOLS, head_count, HEAD_DIM)
        key_part = rounded(jnp.einsum('hqlsk,qlshd->lkhd', grad_five, query_five)).reshape(N_LON, key_total, AW)
        value_part = rounded(jnp.einsum('hqlsk,qlshd->lkhd', probs_five, cotan_five)).reshape(N_LON, key_total, AW)
        key_feat = jnp.einsum('lka,ca->kc', key_part, key_w32, precision=lax.Precision.HIGHEST)
        key_feat = key_feat + jnp.einsum('lka,ca->kc', value_part, value_w32, precision=lax.Precision.HIGHEST)
        placed = jnp.einsum('lqr,qlsc->rlsc', band_onehot, query_feat, precision=lax.Precision.HIGHEST)
        normed_band = key_feat.reshape(PROWS, N_LON, PCOLS, C) + placed
        return (attended_band, normed_band.reshape(PROWS, N_LON * PCOLS, C))
    attended, normed_grad = lax.map(band_attention, (key_rows, value_rows, queries, out_grads, onehot))
    attended = attended.reshape(N_LAT * QSEL, NLON // 4, AW)
    normed_grad = normed_grad.reshape(NLAT // 4, NLON // 4, C)
    pooled_grad = inv_std * (normed_grad - normed_grad.mean(-1, keepdims=True) - standard * (normed_grad * standard).mean(-1, keepdims=True))
    spread_grad = jnp.repeat(jnp.repeat(pooled_grad / 16.0, 4, axis=0), 4, axis=1)
    sigmoid_out = jax.nn.sigmoid(conv_out)
    conv_grad = (spread_grad * (sigmoid_out * (1.0 + conv_out * (1.0 - sigmoid_out)))).astype(jnp.bfloat16)
    flipped = jnp.swapaxes(conv_weight[::-1, ::-1], 2, 3)
    field_grad = conv_wrap(conv_grad, flipped).astype(jnp.bfloat16)
    return (attended, field_grad)
```

```python
import jax
import jax.numpy as jnp
from jax import lax
from jax.experimental import pallas as pl
from jax.experimental.pallas import tpu as pltpu
from jax.sharding import PartitionSpec as P

HEAD_DIM = 64
NORM_EPS = 1e-05
POOL = 4
BF16 = jnp.bfloat16
F32 = jnp.float32

NN = (((1,), (0,)), ((), ()))
NT = (((1,), (1,)), ((), ()))


def mm(a, b, dims=NN):
    return lax.dot_general(a, b, dims, preferred_element_type=F32)


def eye(n):
    rows = lax.broadcasted_iota(jnp.int32, (n, n), 0)
    cols = lax.broadcasted_iota(jnp.int32, (n, n), 1)
    return jnp.where(rows == cols, 1.0, 0.0).astype(BF16)


def make_kernel(lon_n, lat_n, rows, cols, chan, width):
    pr, ps = rows // POOL, cols // POOL
    keys = pr * ps
    heads = width // HEAD_DIM
    hq = heads * ps
    group = chan // HEAD_DIM
    groups = heads // group
    gq = group * ps
    slab_rows = (POOL + 2) * ps
    halo = [
        (0, 0, 1, 0), (1, 0, -1, 0),
        (0, 1, 1, 1), (1, 1, -1, 1),
        (0, 2, 1, -1), (1, 2, -1, -1),
    ]

    def kernel(
        field, conv_w, wq_h, wk_h, wv_h, qrow, ag_h,
        attended, out_grad,
        xr, xs, cg, cw, cwt, wq, wk, wv, ag,
        cout, dsl, nall, ntr, pt, qg, part, recv,
        colmsg, colhalo, obuf, abuf,
        load_sem, out_sem, halo_send, halo_recv, row_send, row_recv,
        g_send, g_recv, s_send, s_recv,
    ):
        lon = lax.axis_index("lon")
        lat = lax.axis_index("lat")

        def at(dlon, dlat):
            return {
                "lon": lax.rem(lon + dlon + lon_n, lon_n),
                "lat": lax.rem(lat + dlat + lat_n, lat_n),
            }

        loads = [
            pltpu.make_async_copy(field, xr.at[pl.ds(1, rows)], load_sem.at[0]),
            pltpu.make_async_copy(conv_w, cw, load_sem.at[1]),
            pltpu.make_async_copy(ag_h.at[0], ag, load_sem.at[2]),
            pltpu.make_async_copy(wv_h, wv, load_sem.at[3]),
            pltpu.make_async_copy(wq_h, wq, load_sem.at[4]),
            pltpu.make_async_copy(wk_h, wk, load_sem.at[5]),
        ]
        for load in loads:
            load.start()

        barrier = pltpu.get_barrier_semaphore()

        def greet(d, _):
            pl.semaphore_signal(
                barrier, inc=1, device_id=at(d, 0), device_id_type=pl.DeviceIdType.MESH
            )
            return 0

        lax.fori_loop(1, lon_n, greet, 0)
        for dlat in (-1, 1):
            for dlon in (-1, 0, 1):
                pl.semaphore_signal(
                    barrier, inc=1, device_id=at(dlon, dlat), device_id_type=pl.DeviceIdType.MESH
                )

        def column_copies(phase):
            return [
                pltpu.make_async_remote_copy(
                    src_ref=colmsg.at[phase, side],
                    dst_ref=colhalo.at[phase, side, place],
                    send_sem=halo_send.at[phase, k],
                    recv_sem=halo_recv.at[phase, k],
                    device_id=at(dlon, dlat),
                    device_id_type=pl.DeviceIdType.MESH,
                )
                for k, (side, place, dlon, dlat) in enumerate(halo)
            ]

        def row_copies(phase, up_src, up_dst, down_src, down_dst):
            return [
                pltpu.make_async_remote_copy(
                    src_ref=src,
                    dst_ref=dst,
                    send_sem=row_send.at[phase, k],
                    recv_sem=row_recv.at[phase, k],
                    device_id=at(0, dlat),
                    device_id_type=pl.DeviceIdType.MESH,
                )
                for k, (src, dst, dlat) in enumerate(
                    ((up_src, up_dst, -1), (down_src, down_dst, 1))
                )
            ]

        loads[0].wait()
        for i in range(rows):
            colmsg[0, 0, i : i + 1, :] = xr[1 + i, cols - 16 : cols, :].astype(F32)[15:16]
            colmsg[0, 1, i : i + 1, :] = xr[1 + i, 0:16, :].astype(F32)[0:1]
        pl.semaphore_wait(barrier, lon_n - 1 + 6)
        cols_out = column_copies(0)
        rows_out = row_copies(0, xr.at[1], xr.at[rows + 1], xr.at[rows], xr.at[0])
        for c in rows_out + cols_out:
            c.start()

        prow = lax.broadcasted_iota(jnp.int32, (slab_rows, cols), 0)
        pcol = lax.broadcasted_iota(jnp.int32, (slab_rows, cols), 1)
        spread = jnp.where(
            pcol == (prow % ps) * POOL + prow // ps - 1, 1.0, 0.0
        ).astype(BF16)
        srow = lax.broadcasted_iota(jnp.int32, (slab_rows, chan), 0)

        def slabs(r, left, right, zero):
            y = mm(spread, xr[r])
            y = jnp.where(srow == 0, left, jnp.where(srow == slab_rows - 1, right, y))
            if zero is not None:
                y = jnp.where(zero, 0.0, y)
            xs[r] = y.astype(BF16)

        hrow = lax.broadcasted_iota(jnp.int32, (gq, chan), 0) // ps
        hcol = lax.broadcasted_iota(jnp.int32, (gq, chan), 1) // HEAD_DIM
        head_mask = hrow == hcol

        def absorb(x, w_ref, g, scale):
            part_g = x[:, g * chan : (g + 1) * chan]
            wide = jnp.where(head_mask, jnp.concatenate([part_g] * group, axis=0), 0.0)
            y = mm(wide.astype(BF16), w_ref[:, g * chan : (g + 1) * chan], NT)
            return (y * scale).astype(BF16) if scale != 1.0 else y.astype(BF16)

        loads[2].wait()
        loads[3].wait()
        for g in range(groups):
            qg[g * gq : (g + 1) * gq, :] = absorb(ag[...].astype(F32), wv, g, 1.0)

        for c in cols_out:
            c.wait()
        for i in range(rows):
            slabs(
                1 + i,
                colhalo[0, 0, 0, i : i + 1, :],
                colhalo[0, 1, 0, i : i + 1, :],
                None,
            )
        for c in rows_out:
            c.wait()
        slabs(
            0,
            colhalo[0, 0, 1, rows - 1 : rows, :],
            colhalo[0, 1, 1, rows - 1 : rows, :],
            lat == 0,
        )
        slabs(
            rows + 1,
            colhalo[0, 0, 2, 0:1, :],
            colhalo[0, 1, 2, 0:1, :],
            lat == lat_n - 1,
        )

        loads[1].wait()
        pooled = []
        for p in range(pr):
            r0 = p * POOL
            acc = None
            for a in range(3):
                lhs = jnp.concatenate(
                    [
                        xs[r0 + a : r0 + a + POOL, b * ps : b * ps + cols, :].reshape(
                            POOL * cols, chan
                        )
                        for b in range(3)
                    ],
                    axis=1,
                )
                term = mm(lhs, cw[a].reshape(3 * chan, chan))
                acc = term if acc is None else acc + term
            cout[r0 * cols : (r0 + POOL) * cols, :] = acc
            act = acc * (0.5 * jnp.tanh(0.5 * acc) + 0.5)
            pooled.append(act.reshape(POOL * POOL, ps, chan).sum(axis=0) * (1.0 / (POOL * POOL)))
        pooled = jnp.concatenate(pooled, axis=0)
        centred = pooled - pooled.mean(-1, keepdims=True)
        inv_std = lax.rsqrt((centred * centred).mean(-1, keepdims=True) + NORM_EPS)
        standard = centred * inv_std
        normed = standard.astype(BF16)
        nall[0] = normed

        def gather_copy(d):
            return pltpu.make_async_remote_copy(
                src_ref=nall.at[0],
                dst_ref=nall.at[d],
                send_sem=g_send.at[d],
                recv_sem=g_recv.at[d],
                device_id=at(d, 0),
                device_id_type=pl.DeviceIdType.MESH,
            )

        def run(fn):
            def body(d, _):
                fn(d)
                return 0

            lax.fori_loop(1, lon_n, body, 0)

        run(lambda d: gather_copy(d).start())

        first = qrow[...] == 0
        chosen = jnp.where(first, standard[:ps], standard[ps:]).astype(BF16)
        loads[4].wait()
        loads[5].wait()
        q = mm(chosen, wq[...]).astype(BF16).astype(F32)
        for g in range(groups):
            qg[hq + g * gq : hq + (g + 1) * gq, :] = absorb(q, wk, g, HEAD_DIM**-0.5)
        for i in range(rows):
            v = cout[i * cols : (i + 1) * cols, :]
            sig = 0.5 * jnp.tanh(0.5 * v) + 0.5
            dsl[i * cols : (i + 1) * cols, :] = sig * (1.0 + v * (1.0 - sig)) * (
                1.0 / (POOL * POOL)
            )
        ident = eye(chan)
        for a in range(3):
            for b in range(3):
                cwt[a, b] = mm(ident, cw[a, b], NT).astype(BF16)

        run(lambda d: gather_copy(d).wait())

        nv = nall[...].reshape(lon_n * keys, chan)
        ntr[...] = mm(ident, nv, NT).astype(BF16)
        blk = min(256, hq)
        for h0 in range(0, hq, blk):
            s = mm(nv, qg[hq + h0 : hq + h0 + blk, :], NT)
            e = jnp.exp(s - s.max(axis=0, keepdims=True))
            prob = e * (1.0 / e.sum(axis=0, keepdims=True))
            dp = mm(nv, qg[h0 : h0 + blk, :], NT)
            delta = (prob * dp).sum(axis=0, keepdims=True)
            pt[:, h0 : h0 + blk] = prob.astype(BF16)
            pt[:, hq + h0 : hq + h0 + blk] = (prob * (dp - delta)).astype(BF16)

        def scatter_copy(d):
            return pltpu.make_async_remote_copy(
                src_ref=part.at[d],
                dst_ref=recv.at[d],
                send_sem=s_send.at[d],
                recv_sem=s_recv.at[d],
                device_id=at(lon_n - d, 0),
                device_id_type=pl.DeviceIdType.MESH,
            )

        step = 4
        own = None
        for d0 in range(0, lon_n, step):
            y = mm(pt[d0 * keys : (d0 + step) * keys, :], qg[...])
            if d0 == 0:
                own = y[:keys]
            part[d0 : d0 + step] = y.astype(BF16).reshape(step, keys, chan)
            for d in range(max(d0, 1), d0 + step):
                scatter_copy(d).start()

        ident_g = eye(gq)
        qfeat = jnp.zeros((ps, chan), F32)
        for g in range(groups):
            for which in range(2):
                c0 = which * hq + g * gq
                u = mm(ntr[...], pt[:, c0 : c0 + gq]).astype(BF16)
                u = mm(ident_g, u, NT).astype(BF16)
                w = (wv, wk)[which][:, g * chan : (g + 1) * chan]
                y = jnp.where(head_mask, mm(u, w), 0.0).reshape(group, ps, chan).sum(axis=0)
                if which == 0:
                    abuf[:, g * chan : (g + 1) * chan] = y.astype(BF16)
                else:
                    y = (y * HEAD_DIM**-0.5).astype(BF16)
                    qfeat = qfeat + mm(y, wq[:, g * chan : (g + 1) * chan], NT)
        att_out = pltpu.make_async_copy(abuf, attended.at[0], out_sem.at[rows])
        att_out.start()

        zero = jnp.zeros_like(qfeat)
        total = own + jnp.concatenate(
            [jnp.where(first, qfeat, zero), jnp.where(first, zero, qfeat)], axis=0
        )
        run(lambda d: scatter_copy(d).wait())
        total = total + recv[1:].astype(F32).sum(axis=0)

        pgrad = inv_std * (
            total
            - total.mean(-1, keepdims=True)
            - standard * (total * standard).mean(-1, keepdims=True)
        )

        edge = lax.broadcasted_iota(jnp.int32, (ps, chan), 0)
        ends = {}

        def grad_row(i):
            pg = pgrad[(i // POOL) * ps : (i // POOL + 1) * ps]
            for t in range(POOL):
                at_row = i * cols + t * ps
                slab = (pg * dsl[at_row : at_row + ps, :]).astype(BF16)
                cg[1 + i, (t + 1) * ps : (t + 2) * ps, :] = slab
                if t == 0:
                    colmsg[1, 1, i : i + 1, :] = slab.astype(F32)[0:1]
                    ends[i, 0] = slab
                if t == POOL - 1:
                    colmsg[1, 0, i : i + 1, :] = slab.astype(F32)[ps - 1 : ps]
                    ends[i, 1] = slab

        mid = pl.ds(ps, cols)
        rows_out = row_copies(
            1, cg.at[1, mid], cg.at[rows + 1, mid], cg.at[rows, mid], cg.at[0, mid]
        )
        grad_row(0)
        rows_out[0].start()
        grad_row(rows - 1)
        rows_out[1].start()
        for i in range(1, rows - 1):
            grad_row(i)
        cols_out = column_copies(1)
        for c in cols_out:
            c.start()

        def edges(r, first_slab, last_slab, left, right):
            lo = pltpu.roll(last_slab.astype(F32), 1, 0)
            hi = pltpu.roll(first_slab.astype(F32), ps - 1, 0)
            cg[r, 0:ps, :] = jnp.where(edge == 0, left, lo).astype(BF16)
            cg[r, slab_rows - ps : slab_rows, :] = jnp.where(
                edge == ps - 1, right, hi
            ).astype(BF16)

        for c in cols_out:
            c.wait()
        for i in range(rows):
            edges(
                1 + i,
                ends[i, 0],
                ends[i, 1],
                colhalo[1, 0, 0, i : i + 1, :],
                colhalo[1, 1, 0, i : i + 1, :],
            )
        for c in rows_out:
            c.wait()
        for r, place, pick, pole in ((0, 1, rows - 1, 0), (rows + 1, 2, 0, lat_n - 1)):
            edges(
                r,
                cg[r, ps : 2 * ps, :],
                cg[r, POOL * ps : (POOL + 1) * ps, :],
                colhalo[1, 0, place, pick : pick + 1, :],
                colhalo[1, 1, place, pick : pick + 1, :],
            )
            cg[r] = jnp.where(lat == pole, 0.0, cg[r].astype(F32)).astype(BF16)

        prow = lax.broadcasted_iota(jnp.int32, (cols, cols), 0)
        pcol = lax.broadcasted_iota(jnp.int32, (cols, cols), 1)
        weave = jnp.where(prow == (pcol % ps) * POOL + pcol // ps, 1.0, 0.0).astype(BF16)
        stores = []
        for p in range(pr):
            r0 = p * POOL
            acc = None
            for a in range(3):
                lhs = jnp.concatenate(
                    [
                        cg[
                            r0 + 2 - a : r0 + 2 - a + POOL, (2 - b) * ps : (2 - b) * ps + cols, :
                        ].reshape(POOL * cols, chan)
                        for b in range(3)
                    ],
                    axis=1,
                )
                term = mm(lhs, cwt[a].reshape(3 * chan, chan))
                acc = term if acc is None else acc + term
            acc = acc.astype(BF16)
            for i in range(POOL):
                obuf[r0 + i] = mm(weave, acc[i * cols : (i + 1) * cols]).astype(BF16)
                store = pltpu.make_async_copy(
                    obuf.at[r0 + i], out_grad.at[r0 + i], out_sem.at[r0 + i]
                )
                store.start()
                stores.append(store)
        att_out.wait()
        for store in stores:
            store.wait()

    return kernel


def solution(mesh):
    lon_n, lat_n = mesh.shape["lon"], mesh.shape["lat"]

    def on_device(field, conv_w, wq, wk, wv, query_rows, attended_grad):
        rows, cols, chan = field.shape
        width = wq.shape[1]
        pr, ps = rows // POOL, cols // POOL
        keys = pr * ps
        hq = (width // HEAD_DIM) * ps
        slab_rows = (POOL + 2) * ps
        any_spec = pl.BlockSpec(memory_space=pl.ANY)
        vmem = pl.BlockSpec(memory_space=pltpu.VMEM)
        return pl.pallas_call(
            make_kernel(lon_n, lat_n, rows, cols, chan, width),
            out_shape=(
                jax.ShapeDtypeStruct(attended_grad.shape, BF16),
                jax.ShapeDtypeStruct(field.shape, BF16),
            ),
            in_specs=[any_spec] * 5 + [vmem, any_spec],
            out_specs=(any_spec, any_spec),
            scratch_shapes=[
                pltpu.VMEM((rows + 2, cols, chan), BF16),
                pltpu.VMEM((rows + 2, slab_rows, chan), BF16),
                pltpu.VMEM((rows + 2, slab_rows, chan), BF16),
                pltpu.VMEM((3, 3, chan, chan), BF16),
                pltpu.VMEM((3, 3, chan, chan), BF16),
                pltpu.VMEM((chan, width), BF16),
                pltpu.VMEM((chan, width), BF16),
                pltpu.VMEM((chan, width), BF16),
                pltpu.VMEM((ps, width), BF16),
                pltpu.VMEM((rows * cols, chan), F32),
                pltpu.VMEM((rows * cols, chan), F32),
                pltpu.VMEM((lon_n, keys, chan), BF16),
                pltpu.VMEM((chan, lon_n * keys), BF16),
                pltpu.VMEM((lon_n * keys, 2 * hq), BF16),
                pltpu.VMEM((2 * hq, chan), BF16),
                pltpu.VMEM((lon_n, keys, chan), BF16),
                pltpu.VMEM((lon_n, keys, chan), BF16),
                pltpu.VMEM((2, 2, rows, chan), F32),
                pltpu.VMEM((2, 2, 3, rows, chan), F32),
                pltpu.VMEM((rows, cols, chan), BF16),
                pltpu.VMEM((ps, width), BF16),
                pltpu.SemaphoreType.DMA((6,)),
                pltpu.SemaphoreType.DMA((rows + 1,)),
                pltpu.SemaphoreType.DMA((2, 6)),
                pltpu.SemaphoreType.DMA((2, 6)),
                pltpu.SemaphoreType.DMA((2, 2)),
                pltpu.SemaphoreType.DMA((2, 2)),
                pltpu.SemaphoreType.DMA((lon_n,)),
                pltpu.SemaphoreType.DMA((lon_n,)),
                pltpu.SemaphoreType.DMA((lon_n,)),
                pltpu.SemaphoreType.DMA((lon_n,)),
            ],
            compiler_params=pltpu.CompilerParams(
                collective_id=0, has_side_effects=True, vmem_limit_bytes=56 * 1024 * 1024
            ),
        )(field, conv_w, wq, wk, wv, query_rows.reshape(1, 1), attended_grad)

    return jax.shard_map(
        on_device,
        mesh=mesh,
        in_specs=(
            P("lat", "lon", None),
            P(),
            P(),
            P(),
            P(),
            P("lat", "lon", None),
            P("lat", "lon", None),
        ),
        out_specs=(P("lat", "lon", None), P("lat", "lon", None)),
        check_vma=False,
    )
```

```python
import itertools

import jax
import jax.numpy as jnp
from jax import lax
from jax.experimental import pallas as pl
from jax.experimental.pallas import tpu as pltpu
from jax.sharding import PartitionSpec as P

HEAD_DIM = 64
NORM_EPS = 1e-05
POOL = 4
BF16 = jnp.bfloat16
F32 = jnp.float32
MESH = pl.DeviceIdType.MESH

NN = (((1,), (0,)), ((), ()))
NT = (((1,), (1,)), ((), ()))


def mm(a, b, dims=NN):
    return lax.dot_general(a, b, dims, preferred_element_type=F32)


def eye(n):
    rows = lax.broadcasted_iota(jnp.int32, (n, n), 0)
    cols = lax.broadcasted_iota(jnp.int32, (n, n), 1)
    return jnp.where(rows == cols, 1.0, 0.0).astype(BF16)


def windows(ref, pieces, ps, flip):
    chan = ref.shape[-1]
    stacked = []
    for r0, r1, t0, t1 in pieces:
        taps = []
        for a in range(3):
            for b in range(3):
                da, db = (2 - a, 2 - b) if flip else (a, b)
                taps.append(
                    ref[r0 + da : r1 + da, (t0 + db) * ps : (t1 + db) * ps, :].reshape(
                        (r1 - r0) * (t1 - t0) * ps, chan
                    )
                )
        stacked.append(jnp.concatenate(taps, axis=1))
    return jnp.concatenate(stacked, axis=0) if len(stacked) > 1 else stacked[0]


def taps_nt(w_ref):
    return jnp.concatenate([w_ref[a, b] for a in range(3) for b in range(3)], axis=1)


def pieces_of(rows):
    inner = [(1, rows - 1, 1, POOL - 1)]
    outer = [
        (1, rows - 1, 0, 1),
        (1, rows - 1, POOL - 1, POOL),
        (0, 1, 0, POOL),
        (rows - 1, rows, 0, POOL),
    ]
    return inner, outer


def slabs_of(pieces):
    return [(r, t) for r0, r1, t0, t1 in pieces for r in range(r0, r1) for t in range(t0, t1)]


def make_kernel(lon_n, lat_n, rows, cols, chan, width):
    pr, ps = rows // POOL, cols // POOL
    keys = pr * ps
    heads = width // HEAD_DIM
    hq = heads * ps
    group = chan // HEAD_DIM
    groups = heads // group
    gq = group * ps
    slab_rows = (POOL + 2) * ps
    chips = lon_n // 2
    inner, outer = pieces_of(rows)
    half = ps // 2
    halo = [
        (0, 0, 1, 0), (1, 0, -1, 0),
        (0, 1, 1, 1), (1, 1, -1, 1),
        (0, 2, 1, -1), (1, 2, -1, -1),
    ]

    def kernel(
        field, conv_w, wq_h, wk_h, wv_h, qrow, ag_h,
        attended, cg, gin,
        xr, xs, cw, wq, wk, wv, ag,
        cout, dsl, nall, chosen, ntr, ex, dpr, pt, utb, gall, part, recv,
        stat, joined, colmsg, colhalo, dslrow, dslhalo, pgb, pgmid, pgcor, pgrow,
        load_sem, send_sem, recv_sem,
    ):
        lon = lax.axis_index("lon")
        lat = lax.axis_index("lat")
        count = itertools.count()

        def at(dlon, dlat):
            return {
                "lon": lax.rem(lon + dlon + lon_n, lon_n),
                "lat": lax.rem(lat + dlat + lat_n, lat_n),
            }

        sibling = {"lon": lon + 1 - 2 * lax.rem(lon, 2), "lat": lat}

        def remote(src, dst, device):
            k = next(count)
            return pltpu.make_async_remote_copy(
                src_ref=src,
                dst_ref=dst,
                send_sem=send_sem.at[k],
                recv_sem=recv_sem.at[k],
                device_id=device,
                device_id_type=MESH,
            )

        def start(copies):
            for c in copies:
                c.start()

        def wait(copies):
            for c in copies:
                c.wait()

        loads = [
            pltpu.make_async_copy(field, xr.at[pl.ds(1, rows)], load_sem.at[0]),
            pltpu.make_async_copy(conv_w, cw, load_sem.at[1]),
            pltpu.make_async_copy(ag_h.at[0], ag.at[0], load_sem.at[2]),
            pltpu.make_async_copy(wv_h, wv, load_sem.at[3]),
            pltpu.make_async_copy(wq_h, wq, load_sem.at[4]),
            pltpu.make_async_copy(wk_h, wk, load_sem.at[5]),
        ]
        loads[0].start()

        barrier = pltpu.get_barrier_semaphore()
        friends = [(0, -1), (0, 1)] + [(dlon, dlat) for _, _, dlon, dlat in halo]
        friends += [(2 * e, 0) for e in range(1, chips)]
        for dlon, dlat in friends:
            pl.semaphore_signal(barrier, inc=1, device_id=at(dlon, dlat), device_id_type=MESH)
        start(loads[1:])

        def columns(phase):
            return [
                remote(colmsg.at[phase, side], colhalo.at[phase, side, place], at(dlon, dlat))
                for side, place, dlon, dlat in halo
            ]

        loads[0].wait()
        for i in range(rows):
            colmsg[0, 0, i : i + 1, :] = xr[1 + i, cols - 16 : cols, :].astype(F32)[15:16]
            colmsg[0, 1, i : i + 1, :] = xr[1 + i, 0:16, :].astype(F32)[0:1]
        pl.semaphore_wait(barrier, len(friends))
        field_rows = [
            remote(field.at[0], xr.at[rows + 1], at(0, -1)),
            remote(field.at[rows - 1], xr.at[0], at(0, 1)),
        ]
        field_cols = columns(0)
        grads = remote(ag_h.at[0], ag.at[1], sibling)
        start(field_rows + field_cols + [grads])

        prow = lax.broadcasted_iota(jnp.int32, (slab_rows, cols), 0)
        pcol = lax.broadcasted_iota(jnp.int32, (slab_rows, cols), 1)
        spread = jnp.where(
            pcol == lax.rem(prow, ps) * POOL + lax.div(prow, ps) - 1, 1.0, 0.0
        ).astype(BF16)
        tile_row = lax.broadcasted_iota(jnp.int32, (16, chan), 0)

        def patch(ref, r, left, right):
            end = slab_rows - 16
            ref[r, 0:16, :] = jnp.where(tile_row == 0, left, ref[r, 0:16, :].astype(F32)).astype(
                BF16
            )
            ref[r, end:slab_rows, :] = jnp.where(
                tile_row == 15, right, ref[r, end:slab_rows, :].astype(F32)
            ).astype(BF16)

        for i in range(rows):
            xs[1 + i] = mm(spread, xr[1 + i]).astype(BF16)

        def convolve(pieces):
            y = mm(windows(xs, pieces, ps, False), cw[...].reshape(9 * chan, chan))
            for k, (r, t) in enumerate(slabs_of(pieces)):
                at_row = r * cols + t * ps
                cout[at_row : at_row + ps, :] = y[k * ps : (k + 1) * ps]

        loads[1].wait()
        convolve(inner)

        hrow = lax.div(lax.broadcasted_iota(jnp.int32, (gq, chan), 0), ps)
        hcol = lax.div(lax.broadcasted_iota(jnp.int32, (gq, chan), 1), HEAD_DIM)
        head_mask = hrow == hcol

        def absorb(x, w_ref, base, scale):
            for g in range(groups):
                x_g = x[:, g * chan : (g + 1) * chan]
                wide = jnp.where(head_mask, jnp.concatenate([x_g] * group, axis=0), 0.0)
                y = mm(wide.astype(BF16), w_ref[:, g * chan : (g + 1) * chan], NT)
                y = y * scale if scale != 1.0 else y
                gall[base + g * gq : base + (g + 1) * gq, :] = y.astype(BF16)

        loads[2].wait()
        loads[3].wait()
        absorb(ag[0].astype(F32), wv, 0, 1.0)

        wait(field_cols)
        for i in range(rows):
            patch(
                xs, 1 + i, colhalo[0, 0, 0, i : i + 1, :], colhalo[0, 1, 0, i : i + 1, :]
            )
        wait(field_rows)
        for r, place, pick, pole in ((0, 1, rows - 1, 0), (rows + 1, 2, 0, lat_n - 1)):
            xs[r] = mm(spread, xr[r]).astype(BF16)
            patch(
                xs,
                r,
                colhalo[0, 0, place, pick : pick + 1, :],
                colhalo[0, 1, place, pick : pick + 1, :],
            )
            xs[r] = jnp.where(lat == pole, 0.0, xs[r].astype(F32)).astype(BF16)
        convolve(outer)

        pooled = []
        for p in range(pr):
            v = cout[p * POOL * cols : (p + 1) * POOL * cols, :]
            act = v * (0.5 * jnp.tanh(0.5 * v) + 0.5)
            pooled.append(act.reshape(POOL * POOL, ps, chan).sum(axis=0) * (1.0 / (POOL * POOL)))
        pooled = jnp.concatenate(pooled, axis=0)
        centred = pooled - pooled.mean(-1, keepdims=True)
        inv_std = lax.rsqrt((centred * centred).mean(-1, keepdims=True) + NORM_EPS)
        standard = centred * inv_std
        nall[0] = standard.astype(BF16)
        first = qrow[0] == 0
        chosen[0] = jnp.where(first, standard[:ps], standard[ps:]).astype(BF16)

        order = [e for e in range(1, chips, 2)] + [e for e in range(2, chips, 2)]
        gathers = [remote(nall.at[0], nall.at[e], at(2 * e, 0)) for e in order]
        picks = remote(chosen.at[0], chosen.at[1], sibling)
        start([picks] + gathers)

        loads[4].wait()
        loads[5].wait()
        picks.wait()
        q = mm(chosen[...].reshape(2 * ps, chan), wq[...]).astype(BF16).astype(F32)
        absorb(q[:ps], wk, 2 * hq, HEAD_DIM**-0.5)
        absorb(q[ps:], wk, 3 * hq, HEAD_DIM**-0.5)
        grads.wait()
        absorb(ag[1].astype(F32), wv, hq, 1.0)
        for i in range(rows):
            v = cout[i * cols : (i + 1) * cols, :]
            sig = 0.5 * jnp.tanh(0.5 * v) + 0.5
            d = sig * (1.0 + v * (1.0 - sig)) * (1.0 / (POOL * POOL))
            dsl[i * cols : (i + 1) * cols, :] = d
            colmsg[1, 1, i : i + 1, :] = d[0:1]
            colmsg[1, 0, i : i + 1, :] = d[cols - 1 : cols]
            if i == 0:
                dslrow[0] = d.astype(BF16)
            if i == rows - 1:
                dslrow[1] = d.astype(BF16)
        ident = eye(chan)

        wait(gathers)
        slope_rows = [
            remote(dslrow.at[0], dslhalo.at[1], at(0, -1)),
            remote(dslrow.at[1], dslhalo.at[0], at(0, 1)),
        ]
        slope_cols = columns(1)
        start(slope_rows + slope_cols)

        nv = nall[...].reshape(chips * keys, chan)
        blk = chan
        for h0 in range(0, 2 * hq, blk):
            s = mm(nv, gall[2 * hq + h0 : 2 * hq + h0 + blk, :], NT)
            top = s.max(axis=0, keepdims=True)
            e = jnp.exp(s - top)
            dp = mm(nv, gall[h0 : h0 + blk, :], NT)
            ex[:, h0 : h0 + blk] = e
            dpr[:, h0 : h0 + blk] = dp
            stat[0, 0:1, h0 : h0 + blk] = top
            stat[0, 1:2, h0 : h0 + blk] = e.sum(axis=0, keepdims=True)
            stat[0, 2:3, h0 : h0 + blk] = (e * dp).sum(axis=0, keepdims=True)
        stats = remote(stat.at[0], stat.at[1], sibling)
        stats.start()
        ntr[...] = mm(ident, nv, NT).astype(BF16)
        stats.wait()
        for h0 in range(0, 2 * hq, blk):
            o0 = (h0 + hq) % (2 * hq)
            top, size, dot = (stat[0, k : k + 1, h0 : h0 + blk] for k in range(3))
            top2, size2, dot2 = (stat[1, k : k + 1, o0 : o0 + blk] for k in range(3))
            peak = jnp.maximum(top, top2)
            f, f2 = jnp.exp(top - peak), jnp.exp(top2 - peak)
            inv = 1.0 / (size * f + size2 * f2)
            delta = (dot * f + dot2 * f2) * inv
            prob = ex[:, h0 : h0 + blk] * (f * inv)
            pt[:, h0 : h0 + blk] = prob.astype(BF16)
            pt[:, 2 * hq + h0 : 2 * hq + h0 + blk] = (
                prob * (dpr[:, h0 : h0 + blk] - delta)
            ).astype(BF16)

        scatters = {}
        own = None
        step = chips // 2
        for d0 in (step, 0):
            y = mm(pt[d0 * keys : (d0 + step) * keys, :], gall[...])
            if d0 == 0:
                own = y[:keys]
            part[d0 : d0 + step] = y.astype(BF16).reshape(step, keys, chan)
            for e in range(max(d0, 1), d0 + step):
                scatters[e] = remote(part.at[e], recv.at[e], at(-2 * e, 0))
                scatters[e].start()

        utb[...] = mm(ntr[...], pt[...]).astype(BF16)
        ident_g = eye(gq)
        mine = None
        for owner in (1, 0):
            outs = []
            qfeat = jnp.zeros((ps, chan), F32)
            for g in range(groups):
                for which in range(2):
                    c0 = (2 * which + owner) * hq + g * gq
                    u = mm(ident_g, utb[:, c0 : c0 + gq], NT).astype(BF16)
                    w = (wv, wk)[which][:, g * chan : (g + 1) * chan]
                    y = jnp.where(head_mask, mm(u, w), 0.0).reshape(group, ps, chan).sum(axis=0)
                    if which == 0:
                        outs.append(y)
                    else:
                        y = (y * HEAD_DIM**-0.5).astype(BF16)
                        qfeat = qfeat + mm(y, wq[:, g * chan : (g + 1) * chan], NT)
            if owner == 1:
                for g in range(groups):
                    joined[0, :, g * chan : (g + 1) * chan] = outs[g]
                joined[0, :, width : width + chan] = qfeat
                joins = remote(joined.at[0], joined.at[1], sibling)
                joins.start()
            else:
                mine = (outs, qfeat)
        joins.wait()
        outs, qfeat = mine
        for g in range(groups):
            cell = slice(g * chan, (g + 1) * chan)
            attended[0, :, cell] = (outs[g] + joined[1, :, cell]).astype(BF16)
        qfeat = qfeat + joined[1, :, width : width + chan]

        zero = jnp.zeros_like(qfeat)
        total = own + jnp.concatenate(
            [jnp.where(first, qfeat, zero), jnp.where(first, zero, qfeat)], axis=0
        )
        wait(slope_rows + slope_cols)
        wait(scatters.values())
        total = total + recv[1:].astype(F32).sum(axis=0)
        pgrad = inv_std * (
            total
            - total.mean(-1, keepdims=True)
            - standard * (total * standard).mean(-1, keepdims=True)
        )
        pgb[...] = pgrad.astype(BF16).reshape(pr, ps, chan)
        sides = (pl.ds(ps - half, half), pl.ds(0, half))
        pg_rows = [
            remote(pgb.at[0], pgrow.at[1], at(0, -1)),
            remote(pgb.at[pr - 1], pgrow.at[0], at(0, 1)),
        ]
        pg_cols = []
        for side, place, dlon, dlat in halo:
            if place == 0:
                src, dst = pgb.at[:, sides[side]], pgmid.at[side]
            else:
                src = pgb.at[pr - 1 if place == 1 else 0, sides[side]]
                dst = pgcor.at[side, place - 1]
            pg_cols.append(remote(src, dst, at(dlon, dlat)))
        start(pg_rows + pg_cols)

        def grad_row(r, pg, slope):
            slabs = [pg * slope[t * ps : (t + 1) * ps] for t in range(POOL)]
            cg[r, 0:ps, :] = pltpu.roll(slabs[POOL - 1], 1, 0).astype(BF16)
            cg[r, slab_rows - ps : slab_rows, :] = pltpu.roll(slabs[0], ps - 1, 0).astype(BF16)
            for t in range(POOL):
                cg[r, (t + 1) * ps : (t + 2) * ps, :] = slabs[t].astype(BF16)

        for i in range(rows):
            p = i // POOL
            grad_row(1 + i, pgrad[p * ps : (p + 1) * ps], dsl[i * cols : (i + 1) * cols, :])
        gin[...] = mm(windows(cg, inner, ps, True), taps_nt(cw), NT).astype(BF16)

        wait(pg_cols)
        lefts = [pgmid[0, p].astype(F32)[half - 1 : half] for p in range(pr)]
        rights = [pgmid[1, p].astype(F32)[0:1] for p in range(pr)]
        for i in range(rows):
            patch(
                cg,
                1 + i,
                lefts[i // POOL] * colhalo[1, 0, 0, i : i + 1, :],
                rights[i // POOL] * colhalo[1, 1, 0, i : i + 1, :],
            )
        wait(pg_rows)
        for r, place, pick, pole in ((0, 1, rows - 1, 0), (rows + 1, 2, 0, lat_n - 1)):
            there = jnp.where(lat == pole, 0.0, 1.0)
            grad_row(r, pgrow[place - 1].astype(F32) * there, dslhalo[place - 1].astype(F32))
            patch(
                cg,
                r,
                pgcor[0, place - 1].astype(F32)[half - 1 : half]
                * colhalo[1, 0, place, pick : pick + 1, :]
                * there,
                pgcor[1, place - 1].astype(F32)[0:1]
                * colhalo[1, 1, place, pick : pick + 1, :]
                * there,
            )

    return kernel


def make_final(rows, cols, chan):
    ps = cols // POOL
    inner, outer = pieces_of(rows)

    def kernel(cg, gin, cw, att, attended, out_grad, slab, obuf, sem):
        send_att = pltpu.make_async_copy(att, attended, sem.at[rows])
        send_att.start()
        y = mm(windows(cg, outer, ps, True), taps_nt(cw), NT).astype(BF16)
        where = {}
        for k, rt in enumerate(slabs_of(outer)):
            where[rt] = y[k * ps : (k + 1) * ps]
        for k, rt in enumerate(slabs_of(inner)):
            where[rt] = gin[k * ps : (k + 1) * ps, :]
        prow = lax.broadcasted_iota(jnp.int32, (cols, cols), 0)
        pcol = lax.broadcasted_iota(jnp.int32, (cols, cols), 1)
        weave = jnp.where(
            prow == lax.rem(pcol, ps) * POOL + lax.div(pcol, ps), 1.0, 0.0
        ).astype(BF16)
        stores = [send_att]
        for i in range(rows):
            line = jnp.concatenate([where[i, t] for t in range(POOL)], axis=0)
            obuf[i] = mm(weave, line).astype(BF16)
            store = pltpu.make_async_copy(obuf.at[i], out_grad.at[i], sem.at[i])
            store.start()
            stores.append(store)
        for store in stores:
            store.wait()

    return kernel


def solution(mesh):
    lon_n, lat_n = mesh.shape["lon"], mesh.shape["lat"]

    def on_device(field, conv_w, wq, wk, wv, query_rows, attended_grad):
        rows, cols, chan = field.shape
        width = wq.shape[1]
        pr, ps = rows // POOL, cols // POOL
        keys = pr * ps
        chips = lon_n // 2
        hq = (width // HEAD_DIM) * ps
        slab_rows = (POOL + 2) * ps
        gin_rows = (rows - 2) * (POOL - 2) * ps
        any_spec = pl.BlockSpec(memory_space=pl.ANY)
        vmem = pl.BlockSpec(memory_space=pltpu.VMEM)
        att, cg, gin = pl.pallas_call(
            make_kernel(lon_n, lat_n, rows, cols, chan, width),
            out_shape=(
                pltpu.VMEM(attended_grad.shape, BF16),
                pltpu.VMEM((rows + 2, slab_rows, chan), BF16),
                pltpu.VMEM((gin_rows, chan), BF16),
            ),
            in_specs=[any_spec] * 5 + [vmem, any_spec],
            out_specs=(vmem, vmem, vmem),
            scratch_shapes=[
                pltpu.VMEM((rows + 2, cols, chan), BF16),
                pltpu.VMEM((rows + 2, slab_rows, chan), BF16),
                pltpu.VMEM((3, 3, chan, chan), BF16),
                pltpu.VMEM((chan, width), BF16),
                pltpu.VMEM((chan, width), BF16),
                pltpu.VMEM((chan, width), BF16),
                pltpu.VMEM((2, ps, width), BF16),
                pltpu.VMEM((rows * cols, chan), F32),
                pltpu.VMEM((rows * cols, chan), F32),
                pltpu.VMEM((chips, keys, chan), BF16),
                pltpu.VMEM((2, ps, chan), BF16),
                pltpu.VMEM((chan, chips * keys), BF16),
                pltpu.VMEM((chips * keys, 2 * hq), F32),
                pltpu.VMEM((chips * keys, 2 * hq), F32),
                pltpu.VMEM((chips * keys, 4 * hq), BF16),
                pltpu.VMEM((chan, 4 * hq), BF16),
                pltpu.VMEM((4 * hq, chan), BF16),
                pltpu.VMEM((chips, keys, chan), BF16),
                pltpu.VMEM((chips, keys, chan), BF16),
                pltpu.VMEM((2, 8, 2 * hq), F32),
                pltpu.VMEM((2, ps, width + chan), F32),
                pltpu.VMEM((2, 2, rows, chan), F32),
                pltpu.VMEM((2, 2, 3, rows, chan), F32),
                pltpu.VMEM((2, cols, chan), BF16),
                pltpu.VMEM((2, cols, chan), BF16),
                pltpu.VMEM((pr, ps, chan), BF16),
                pltpu.VMEM((2, pr, ps // 2, chan), BF16),
                pltpu.VMEM((2, 2, ps // 2, chan), BF16),
                pltpu.VMEM((2, ps, chan), BF16),
                pltpu.SemaphoreType.DMA((6,)),
                pltpu.SemaphoreType.DMA((48,)),
                pltpu.SemaphoreType.DMA((48,)),
            ],
            compiler_params=pltpu.CompilerParams(
                collective_id=0, has_side_effects=True, vmem_limit_bytes=55 * 1024 * 1024
            ),
        )(field, conv_w, wq, wk, wv, query_rows, attended_grad)
        return pl.pallas_call(
            make_final(rows, cols, chan),
            out_shape=(
                jax.ShapeDtypeStruct(attended_grad.shape, BF16),
                jax.ShapeDtypeStruct(field.shape, BF16),
            ),
            in_specs=[vmem] * 4,
            out_specs=(any_spec, any_spec),
            scratch_shapes=[
                pltpu.VMEM((POOL * ps, chan), BF16),
                pltpu.VMEM((rows, cols, chan), BF16),
                pltpu.SemaphoreType.DMA((rows + 1,)),
            ],
            compiler_params=pltpu.CompilerParams(vmem_limit_bytes=20 * 1024 * 1024),
        )(cg, gin, conv_w, att)

    return jax.shard_map(
        on_device,
        mesh=mesh,
        in_specs=(
            P("lat", "lon", None),
            P(),
            P(),
            P(),
            P(),
            P("lat", "lon", None),
            P("lat", "lon", None),
        ),
        out_specs=(P("lat", "lon", None), P("lat", "lon", None)),
        check_vma=False,
    )
```

```python
import itertools

import jax
import jax.numpy as jnp
from jax import lax
from jax.experimental import pallas as pl
from jax.experimental.pallas import tpu as pltpu
from jax.sharding import PartitionSpec as P

HEAD_DIM = 64
NORM_EPS = 1e-05
POOL = 4
BF16 = jnp.bfloat16
F32 = jnp.float32
MESH = pl.DeviceIdType.MESH

NN = (((1,), (0,)), ((), ()))
NT = (((1,), (1,)), ((), ()))


def mm(a, b, dims=NN):
    return lax.dot_general(a, b, dims, preferred_element_type=F32)


def eye(n):
    rows = lax.broadcasted_iota(jnp.int32, (n, n), 0)
    cols = lax.broadcasted_iota(jnp.int32, (n, n), 1)
    return jnp.where(rows == cols, 1.0, 0.0).astype(BF16)


def windows(ref, rows, cols, ps, flip):
    chan = ref.shape[-1]
    taps = []
    for a in range(3):
        for b in range(3):
            da, db = (2 - a, 2 - b) if flip else (a, b)
            taps.append(
                ref[da : da + rows, db * ps : db * ps + cols, :].reshape(rows * cols, chan)
            )
    return jnp.concatenate(taps, axis=1)


def silu(v):
    return v * (0.5 * jnp.tanh(0.5 * v) + 0.5)


def make_kernel(lon_n, lat_n, rows, cols, chan, width):
    pr, ps = rows // POOL, cols // POOL
    keys = pr * ps
    heads = width // HEAD_DIM
    hq = heads * ps
    group = chan // HEAD_DIM
    groups = heads // group
    gq = group * ps
    slab_rows = (POOL + 2) * ps
    chips = lon_n // 2
    half = ps // 2
    slot_shift = list(range(0, chips, 2)) + list(range(1, chips, 2))
    split = chips // 2
    halo = [
        (0, 0, 1, 0), (1, 0, -1, 0),
        (0, 1, 1, 1), (1, 1, -1, 1),
        (0, 2, 1, -1), (1, 2, -1, -1),
    ]

    def kernel(
        field, conv_w, wq_h, wk_h, wv_h, qrow, ag_h,
        attended, gout,
        xr, xs, xh, cg, ch, cw, wq, wk, wv, ag,
        cout, ccol, grow, dsl, nall, chosen, ntr, ex, dpr, pt, utb, gall, part, recv,
        stat, joined, colmsg, colhalo, dslrow, dslhalo, pgb, pgmid, pgcor, pgrow,
        load_sem, send_sem, recv_sem,
    ):
        lon = lax.axis_index("lon")
        lat = lax.axis_index("lat")
        count = itertools.count()

        def at(dlon, dlat):
            return {
                "lon": lax.rem(lon + dlon + lon_n, lon_n),
                "lat": lax.rem(lat + dlat + lat_n, lat_n),
            }

        sibling = {"lon": lon + 1 - 2 * lax.rem(lon, 2), "lat": lat}

        def remote(src, dst, device):
            k = next(count)
            return pltpu.make_async_remote_copy(
                src_ref=src,
                dst_ref=dst,
                send_sem=send_sem.at[k],
                recv_sem=recv_sem.at[k],
                device_id=device,
                device_id_type=MESH,
            )

        def start(copies):
            for c in copies:
                c.start()

        def wait(copies):
            for c in copies:
                c.wait()

        loads = [
            pltpu.make_async_copy(field, xr, load_sem.at[0]),
            pltpu.make_async_copy(conv_w, cw, load_sem.at[1]),
            pltpu.make_async_copy(ag_h.at[0], ag.at[0], load_sem.at[2]),
            pltpu.make_async_copy(wv_h, wv, load_sem.at[3]),
            pltpu.make_async_copy(wq_h, wq, load_sem.at[4]),
            pltpu.make_async_copy(wk_h, wk, load_sem.at[5]),
        ]
        loads[0].start()

        barrier = pltpu.get_barrier_semaphore()
        friends = [(0, -1), (0, 1)] + [(dlon, dlat) for _, _, dlon, dlat in halo]
        friends += [(2 * e, 0) for e in range(1, chips)]
        for dlon, dlat in friends:
            pl.semaphore_signal(barrier, inc=1, device_id=at(dlon, dlat), device_id_type=MESH)
        start(loads[1:])

        def columns(phase):
            return [
                remote(colmsg.at[phase, side], colhalo.at[phase, side, place], at(dlon, dlat))
                for side, place, dlon, dlat in halo
            ]

        prow = lax.broadcasted_iota(jnp.int32, (slab_rows, cols), 0)
        pcol = lax.broadcasted_iota(jnp.int32, (slab_rows, cols), 1)
        spread = jnp.where(
            pcol == lax.rem(prow, ps) * POOL + lax.div(prow, ps) - 1, 1.0, 0.0
        ).astype(BF16)
        mid = pl.ds(ps, cols)

        loads[0].wait()
        for i in (0, rows - 1):
            xs[1 + i] = mm(spread, xr[i]).astype(BF16)
        for i in range(rows):
            colmsg[0, 0, i : i + 1, :] = xr[i, cols - 16 : cols, :].astype(F32)[15:16]
            colmsg[0, 1, i : i + 1, :] = xr[i, 0:16, :].astype(F32)[0:1]
        pl.semaphore_wait(barrier, len(friends))
        field_rows = [
            remote(xs.at[1, mid], xh.at[1, mid], at(0, -1)),
            remote(xs.at[rows, mid], xh.at[0, mid], at(0, 1)),
        ]
        field_cols = columns(0)
        grads = remote(ag_h.at[0], ag.at[1], sibling)
        start(field_rows + field_cols + [grads])

        xs[0] = jnp.zeros((slab_rows, chan), BF16)
        xs[rows + 1] = jnp.zeros((slab_rows, chan), BF16)
        for i in range(1, rows - 1):
            xs[1 + i] = mm(spread, xr[i]).astype(BF16)
        loads[1].wait()
        cout[...] = mm(windows(xs, rows, cols, ps, False), cw[...].reshape(9 * chan, chan))
        pooled = []
        for p in range(pr):
            lo, hi = max(p * POOL, 1), min((p + 1) * POOL, rows - 1)
            act = silu(cout[lo * cols : hi * cols, :])
            pooled.append(act.reshape((hi - lo) * POOL, ps, chan).sum(axis=0))
        for i in range(rows):
            ccol[0, i : i + 1, :] = cout[i * cols : i * cols + 1, :]
            ccol[1, i : i + 1, :] = cout[(i + 1) * cols - 1 : (i + 1) * cols, :]

        edge = lax.broadcasted_iota(jnp.int32, (ps, chan), 0)
        line = lax.broadcasted_iota(jnp.int32, (rows, chan), 0)

        def column_taps(cells):
            above = jnp.where(line == 0, 0.0, pltpu.roll(cells, 1, 0))
            below = jnp.where(line == rows - 1, 0.0, pltpu.roll(cells, rows - 1, 0))
            return above, cells, below

        def column_terms(left, right, weights, dims):
            none = jnp.zeros((rows, 3 * chan), F32)
            left, right = jnp.concatenate(left, axis=1), jnp.concatenate(right, axis=1)
            lhs = jnp.concatenate(
                [
                    jnp.concatenate([left, none], axis=1),
                    jnp.concatenate([none, right], axis=1),
                ],
                axis=0,
            ).astype(BF16)
            axis = 1 if dims == NT else 0
            y = mm(lhs, jnp.concatenate(weights, axis=axis), dims)
            return y[:rows], y[rows:]

        def row_slabs(ref, k, first_slab, last_slab, left, right):
            lo = pltpu.roll(last_slab, 1, 0)
            hi = pltpu.roll(first_slab, ps - 1, 0)
            ref[k, 0:ps, :] = jnp.where(edge == 0, left, lo).astype(BF16)
            ref[k, slab_rows - ps : slab_rows, :] = jnp.where(edge == ps - 1, right, hi).astype(
                BF16
            )

        hrow = lax.div(lax.broadcasted_iota(jnp.int32, (gq, chan), 0), ps)
        hcol = lax.div(lax.broadcasted_iota(jnp.int32, (gq, chan), 1), HEAD_DIM)
        head_mask = hrow == hcol

        def absorb(x, w_ref, base, scale):
            for g in range(groups):
                x_g = x[:, g * chan : (g + 1) * chan]
                wide = jnp.where(head_mask, jnp.concatenate([x_g] * group, axis=0), 0.0)
                y = mm(wide.astype(BF16), w_ref[:, g * chan : (g + 1) * chan], NT)
                y = y * scale if scale != 1.0 else y
                gall[base + g * gq : base + (g + 1) * gq, :] = y.astype(BF16)

        loads[2].wait()
        loads[3].wait()
        absorb(ag[0].astype(F32), wv, 0, 1.0)

        wait(field_cols)
        fixes = column_terms(
            column_taps(colhalo[0, 0, 0]),
            column_taps(colhalo[0, 1, 0]),
            [cw[a, 0] for a in range(3)] + [cw[a, 2] for a in range(3)],
            NN,
        )
        for side in range(2):
            before = ccol[side]
            after = before + fixes[side]
            ccol[side] = after
            change = silu(after) - silu(before)
            cell = edge == (0, ps - 1)[side]
            for p in range(pr):
                lo, hi = max(p * POOL, 1), min((p + 1) * POOL, rows - 1)
                part_sum = jnp.where((line >= lo) & (line < hi), change, 0.0).sum(
                    axis=0, keepdims=True
                )
                pooled[p] = pooled[p] + jnp.where(cell, part_sum, 0.0)
        for i in range(rows):
            cout[i * cols : i * cols + 1, :] = ccol[0, i : i + 1, :]
            cout[(i + 1) * cols - 1 : (i + 1) * cols, :] = ccol[1, i : i + 1, :]
        wait(field_rows)
        for k, pick, pole in ((0, rows - 1, 0), (1, 0, lat_n - 1)):
            there = jnp.where(lat == pole, 0.0, 1.0)
            row_slabs(
                xh,
                k,
                xh[k, ps : 2 * ps, :].astype(F32),
                xh[k, POOL * ps : (POOL + 1) * ps, :].astype(F32),
                colhalo[0, 0, 1 + k, pick : pick + 1, :],
                colhalo[0, 1, 1 + k, pick : pick + 1, :],
            )
            lhs = jnp.concatenate([xh[k, b * ps : b * ps + cols, :] for b in range(3)], axis=1)
            fix = mm(lhs, cw[2 * k].reshape(3 * chan, chan)) * there
            i = k * (rows - 1)
            v = cout[i * cols : (i + 1) * cols, :] + fix
            cout[i * cols : (i + 1) * cols, :] = v
            p = k * (pr - 1)
            pooled[p] = pooled[p] + silu(v).reshape(POOL, ps, chan).sum(axis=0)
        pooled = jnp.concatenate(pooled, axis=0) * (1.0 / (POOL * POOL))
        centred = pooled - pooled.mean(-1, keepdims=True)
        inv_std = lax.rsqrt((centred * centred).mean(-1, keepdims=True) + NORM_EPS)
        standard = centred * inv_std
        nall[0] = standard.astype(BF16)
        first = qrow[0] == 0
        chosen[0] = jnp.where(first, standard[:ps], standard[ps:]).astype(BF16)

        gathers = [
            remote(nall.at[0], nall.at[k], at(2 * slot_shift[k], 0)) for k in range(1, chips)
        ]
        picks = remote(chosen.at[0], chosen.at[1], sibling)
        start([picks] + gathers[split - 1 :] + gathers[: split - 1])

        loads[4].wait()
        loads[5].wait()
        picks.wait()
        q = mm(chosen[...].reshape(2 * ps, chan), wq[...]).astype(BF16).astype(F32)
        absorb(q[:ps], wk, 2 * hq, HEAD_DIM**-0.5)
        absorb(q[ps:], wk, 3 * hq, HEAD_DIM**-0.5)
        grads.wait()
        absorb(ag[1].astype(F32), wv, hq, 1.0)
        for i in range(rows):
            v = cout[i * cols : (i + 1) * cols, :]
            sig = 0.5 * jnp.tanh(0.5 * v) + 0.5
            d = sig * (1.0 + v * (1.0 - sig)) * (1.0 / (POOL * POOL))
            dsl[i * cols : (i + 1) * cols, :] = d
            colmsg[1, 1, i : i + 1, :] = d[0:1]
            colmsg[1, 0, i : i + 1, :] = d[cols - 1 : cols]
            if i == 0:
                dslrow[0] = d.astype(BF16)
            if i == rows - 1:
                dslrow[1] = d.astype(BF16)
        ident = eye(chan)

        blk = chan
        half_keys = split * keys

        def score(part_at):
            r0 = part_at * half_keys
            nv = nall[part_at * split : (part_at + 1) * split].reshape(half_keys, chan)
            for h0 in range(0, 2 * hq, blk):
                s = mm(nv, gall[2 * hq + h0 : 2 * hq + h0 + blk, :], NT)
                top = s.max(axis=0, keepdims=True)
                e = jnp.exp(s - top)
                dp = mm(nv, gall[h0 : h0 + blk, :], NT)
                ex[r0 : r0 + half_keys, h0 : h0 + blk] = e
                dpr[r0 : r0 + half_keys, h0 : h0 + blk] = dp
                k = 3 * part_at
                stat[0, k : k + 1, h0 : h0 + blk] = top
                stat[0, k + 1 : k + 2, h0 : h0 + blk] = e.sum(axis=0, keepdims=True)
                stat[0, k + 2 : k + 3, h0 : h0 + blk] = (e * dp).sum(axis=0, keepdims=True)
            return nv

        wait(gathers[: split - 1])
        score(0)
        wait(gathers[split - 1 :])
        score(1)
        stats = remote(stat.at[0], stat.at[1], sibling)
        stats.start()
        slope_rows = [
            remote(dslrow.at[0], dslhalo.at[1], at(0, -1)),
            remote(dslrow.at[1], dslhalo.at[0], at(0, 1)),
        ]
        slope_cols = columns(1)
        start(slope_rows + slope_cols)
        ntr[...] = mm(ident, nall[...].reshape(chips * keys, chan), NT).astype(BF16)
        stats.wait()
        scale = {}
        for h0 in range(0, 2 * hq, blk):
            o0 = (h0 + hq) % (2 * hq)
            tops, sizes, dots = (
                [
                    stat[who, 3 * q + k : 3 * q + k + 1, c0 : c0 + blk]
                    for who, c0 in ((0, h0), (1, o0))
                    for q in range(2)
                ]
                for k in range(3)
            )
            peak = jnp.maximum(jnp.maximum(tops[0], tops[1]), jnp.maximum(tops[2], tops[3]))
            f = [jnp.exp(t - peak) for t in tops]
            inv = 1.0 / sum(a * b for a, b in zip(sizes, f))
            delta = sum(a * b for a, b in zip(dots, f)) * inv
            scale[h0] = (f[0] * inv, f[1] * inv, delta)

        scatters = []
        own = None
        for part_at in (1, 0):
            r0 = part_at * half_keys
            for h0 in range(0, 2 * hq, blk):
                prob = ex[r0 : r0 + half_keys, h0 : h0 + blk] * scale[h0][part_at]
                pt[r0 : r0 + half_keys, h0 : h0 + blk] = prob.astype(BF16)
                pt[r0 : r0 + half_keys, 2 * hq + h0 : 2 * hq + h0 + blk] = (
                    prob * (dpr[r0 : r0 + half_keys, h0 : h0 + blk] - scale[h0][2])
                ).astype(BF16)
            y = mm(pt[r0 : r0 + half_keys, :], gall[...])
            if part_at == 0:
                own = y[:keys]
            part[part_at * split : (part_at + 1) * split] = y.astype(BF16).reshape(
                split, keys, chan
            )
            for k in range(max(part_at * split, 1), (part_at + 1) * split):
                scatters.append(remote(part.at[k], recv.at[k], at(-2 * slot_shift[k], 0)))
                scatters[-1].start()

        utb[...] = mm(ntr[...], pt[...]).astype(BF16)
        ident_g = eye(gq)
        mine = None
        for owner in (1, 0):
            outs = []
            qfeat = jnp.zeros((ps, chan), F32)
            for g in range(groups):
                for which in range(2):
                    c0 = (2 * which + owner) * hq + g * gq
                    u = mm(ident_g, utb[:, c0 : c0 + gq], NT).astype(BF16)
                    w = (wv, wk)[which][:, g * chan : (g + 1) * chan]
                    y = jnp.where(head_mask, mm(u, w), 0.0).reshape(group, ps, chan).sum(axis=0)
                    if which == 0:
                        outs.append(y)
                    else:
                        y = (y * HEAD_DIM**-0.5).astype(BF16)
                        qfeat = qfeat + mm(y, wq[:, g * chan : (g + 1) * chan], NT)
            if owner == 1:
                for g in range(groups):
                    joined[0, :, g * chan : (g + 1) * chan] = outs[g]
                joined[0, :, width : width + chan] = qfeat
                joins = remote(joined.at[0], joined.at[1], sibling)
                joins.start()
            else:
                mine = (outs, qfeat)
        joins.wait()
        outs, qfeat = mine
        for g in range(groups):
            cell = slice(g * chan, (g + 1) * chan)
            attended[0, :, cell] = (outs[g] + joined[1, :, cell]).astype(BF16)
        qfeat = qfeat + joined[1, :, width : width + chan]

        zero = jnp.zeros_like(qfeat)
        total = own + jnp.concatenate(
            [jnp.where(first, qfeat, zero), jnp.where(first, zero, qfeat)], axis=0
        )
        wait(slope_rows + slope_cols)
        wait(scatters)
        total = total + recv[1:].astype(F32).sum(axis=0)
        pgrad = inv_std * (
            total
            - total.mean(-1, keepdims=True)
            - standard * (total * standard).mean(-1, keepdims=True)
        )
        pgb[...] = pgrad.astype(BF16).reshape(pr, ps, chan)
        sides = (pl.ds(ps - half, half), pl.ds(0, half))
        pg_rows = [
            remote(pgb.at[0], pgrow.at[1], at(0, -1)),
            remote(pgb.at[pr - 1], pgrow.at[0], at(0, 1)),
        ]
        pg_cols = []
        for side, place, dlon, dlat in halo:
            if place == 0:
                src, dst = pgb.at[:, sides[side]], pgmid.at[side]
            else:
                src = pgb.at[pr - 1 if place == 1 else 0, sides[side]]
                dst = pgcor.at[side, place - 1]
            pg_cols.append(remote(src, dst, at(dlon, dlat)))
        start(pg_rows + pg_cols)

        cg[0] = jnp.zeros((slab_rows, chan), BF16)
        cg[rows + 1] = jnp.zeros((slab_rows, chan), BF16)
        for i in range(rows):
            p = i // POOL
            pg = pgrad[p * ps : (p + 1) * ps]
            slabs = [
                pg * dsl[i * cols + t * ps : i * cols + (t + 1) * ps, :] for t in range(POOL)
            ]
            for t in range(POOL):
                cg[1 + i, (t + 1) * ps : (t + 2) * ps, :] = slabs[t].astype(BF16)
            row_slabs(cg, 1 + i, slabs[0], slabs[POOL - 1], 0.0, 0.0)
        weights = jnp.concatenate([cw[a, b] for a in range(3) for b in range(3)], axis=1)
        y = mm(windows(cg, rows, cols, ps, True), weights, NT)
        wrow = lax.broadcasted_iota(jnp.int32, (cols, cols), 0)
        wcol = lax.broadcasted_iota(jnp.int32, (cols, cols), 1)
        weave = jnp.where(
            wrow == lax.rem(wcol, ps) * POOL + lax.div(wcol, ps), 1.0, 0.0
        ).astype(BF16)
        grow[0] = y[:cols]
        grow[1] = y[(rows - 1) * cols :]
        for i in range(1, rows - 1):
            gout[i] = mm(weave, y[i * cols : (i + 1) * cols].astype(BF16)).astype(BF16)

        wait(pg_cols)
        halves = []
        for side in range(2):
            at_end = (half - 1, 0)[side]
            cells = [pgmid[side, p].astype(F32)[at_end : at_end + 1] for p in range(pr)]
            cells = jnp.where(line < POOL, cells[0], cells[1])
            halves.append(column_taps(cells * colhalo[1, side, 0])[::-1])
        fixes = column_terms(
            halves[0],
            halves[1],
            [cw[a, 2] for a in range(3)] + [cw[a, 0] for a in range(3)],
            NT,
        )
        tile_row = lax.broadcasted_iota(jnp.int32, (16, chan), 0)
        for i in range(1, rows - 1):
            for side, cut, cell in ((0, slice(0, 16), 0), (1, slice(cols - 16, cols), 15)):
                gout[i, cut, :] = (
                    gout[i, cut, :].astype(F32)
                    + jnp.where(tile_row == cell, fixes[side][i : i + 1], 0.0)
                ).astype(BF16)
        wait(pg_rows)
        for k, pick, pole in ((0, rows - 1, 0), (1, 0, lat_n - 1)):
            there = jnp.where(lat == pole, 0.0, 1.0)
            pg = pgrow[k].astype(F32)
            slope = dslhalo[k].astype(F32)
            slabs = [pg * slope[t * ps : (t + 1) * ps] for t in range(POOL)]
            for t in range(POOL):
                ch[k, (t + 1) * ps : (t + 2) * ps, :] = slabs[t].astype(BF16)
            row_slabs(
                ch,
                k,
                slabs[0],
                slabs[POOL - 1],
                pgcor[0, k].astype(F32)[half - 1 : half]
                * colhalo[1, 0, 1 + k, pick : pick + 1, :],
                pgcor[1, k].astype(F32)[0:1] * colhalo[1, 1, 1 + k, pick : pick + 1, :],
            )
            lhs = jnp.concatenate(
                [ch[k, (2 - b) * ps : (2 - b) * ps + cols, :] for b in range(3)], axis=1
            )
            a = 2 - 2 * k
            y = mm(lhs, jnp.concatenate([cw[a, b] for b in range(3)], axis=1), NT)
            i = k * (rows - 1)
            y = grow[k] + y * there
            first_slab = y[:ps] + jnp.where(edge == 0, fixes[0][i : i + 1], 0.0)
            last_slab = y[cols - ps :] + jnp.where(edge == ps - 1, fixes[1][i : i + 1], 0.0)
            y = jnp.concatenate([first_slab, y[ps : cols - ps], last_slab], axis=0)
            gout[i] = mm(weave, y.astype(BF16)).astype(BF16)

    return kernel


def store_kernel(att, gout, attended, out_grad, sem):
    copies = [
        pltpu.make_async_copy(gout, out_grad, sem.at[0]),
        pltpu.make_async_copy(att, attended, sem.at[1]),
    ]
    for copy in copies:
        copy.start()
    for copy in copies:
        copy.wait()


def solution(mesh):
    lon_n, lat_n = mesh.shape["lon"], mesh.shape["lat"]

    def on_device(field, conv_w, wq, wk, wv, query_rows, attended_grad):
        rows, cols, chan = field.shape
        width = wq.shape[1]
        pr, ps = rows // POOL, cols // POOL
        keys = pr * ps
        chips = lon_n // 2
        hq = (width // HEAD_DIM) * ps
        slab_rows = (POOL + 2) * ps
        any_spec = pl.BlockSpec(memory_space=pl.ANY)
        vmem = pl.BlockSpec(memory_space=pltpu.VMEM)
        att, gout = pl.pallas_call(
            make_kernel(lon_n, lat_n, rows, cols, chan, width),
            out_shape=(
                pltpu.VMEM(attended_grad.shape, BF16),
                pltpu.VMEM(field.shape, BF16),
            ),
            in_specs=[any_spec] * 5 + [vmem, any_spec],
            out_specs=(vmem, vmem),
            scratch_shapes=[
                pltpu.VMEM((rows, cols, chan), BF16),
                pltpu.VMEM((rows + 2, slab_rows, chan), BF16),
                pltpu.VMEM((2, slab_rows, chan), BF16),
                pltpu.VMEM((rows + 2, slab_rows, chan), BF16),
                pltpu.VMEM((2, slab_rows, chan), BF16),
                pltpu.VMEM((3, 3, chan, chan), BF16),
                pltpu.VMEM((chan, width), BF16),
                pltpu.VMEM((chan, width), BF16),
                pltpu.VMEM((chan, width), BF16),
                pltpu.VMEM((2, ps, width), BF16),
                pltpu.VMEM((rows * cols, chan), F32),
                pltpu.VMEM((2, rows, chan), F32),
                pltpu.VMEM((2, cols, chan), F32),
                pltpu.VMEM((rows * cols, chan), F32),
                pltpu.VMEM((chips, keys, chan), BF16),
                pltpu.VMEM((2, ps, chan), BF16),
                pltpu.VMEM((chan, chips * keys), BF16),
                pltpu.VMEM((chips * keys, 2 * hq), F32),
                pltpu.VMEM((chips * keys, 2 * hq), F32),
                pltpu.VMEM((chips * keys, 4 * hq), BF16),
                pltpu.VMEM((chan, 4 * hq), BF16),
                pltpu.VMEM((4 * hq, chan), BF16),
                pltpu.VMEM((chips, keys, chan), BF16),
                pltpu.VMEM((chips, keys, chan), BF16),
                pltpu.VMEM((2, 8, 2 * hq), F32),
                pltpu.VMEM((2, ps, width + chan), F32),
                pltpu.VMEM((2, 2, rows, chan), F32),
                pltpu.VMEM((2, 2, 3, rows, chan), F32),
                pltpu.VMEM((2, cols, chan), BF16),
                pltpu.VMEM((2, cols, chan), BF16),
                pltpu.VMEM((pr, ps, chan), BF16),
                pltpu.VMEM((2, pr, ps // 2, chan), BF16),
                pltpu.VMEM((2, 2, ps // 2, chan), BF16),
                pltpu.VMEM((2, ps, chan), BF16),
                pltpu.SemaphoreType.DMA((6,)),
                pltpu.SemaphoreType.DMA((48,)),
                pltpu.SemaphoreType.DMA((48,)),
            ],
            compiler_params=pltpu.CompilerParams(
                collective_id=0, has_side_effects=True, vmem_limit_bytes=55 * 1024 * 1024
            ),
        )(field, conv_w, wq, wk, wv, query_rows, attended_grad)
        return pl.pallas_call(
            store_kernel,
            out_shape=(
                jax.ShapeDtypeStruct(attended_grad.shape, BF16),
                jax.ShapeDtypeStruct(field.shape, BF16),
            ),
            in_specs=[vmem] * 2,
            out_specs=(any_spec, any_spec),
            scratch_shapes=[pltpu.SemaphoreType.DMA((2,))],
        )(att, gout)

    return jax.shard_map(
        on_device,
        mesh=mesh,
        in_specs=(
            P("lat", "lon", None),
            P(),
            P(),
            P(),
            P(),
            P("lat", "lon", None),
            P("lat", "lon", None),
        ),
        out_specs=(P("lat", "lon", None), P("lat", "lon", None)),
        check_vma=False,
    )
```

```python
import itertools

import jax
import jax.numpy as jnp
from jax import lax
from jax.experimental import pallas as pl
from jax.experimental.pallas import tpu as pltpu
from jax.sharding import PartitionSpec as P

HEAD_DIM = 64
NORM_EPS = 1e-05
POOL = 4
BF16 = jnp.bfloat16
F32 = jnp.float32
MESH = pl.DeviceIdType.MESH

NN = (((1,), (0,)), ((), ()))
NT = (((1,), (1,)), ((), ()))


def mm(a, b, dims=NN):
    return lax.dot_general(a, b, dims, preferred_element_type=F32)


def eye(n):
    rows = lax.broadcasted_iota(jnp.int32, (n, n), 0)
    cols = lax.broadcasted_iota(jnp.int32, (n, n), 1)
    return jnp.where(rows == cols, 1.0, 0.0).astype(BF16)


def windows(ref, rows, cols, ps, flip):
    chan = ref.shape[-1]
    taps = []
    for a in range(3):
        for b in range(3):
            da, db = (2 - a, 2 - b) if flip else (a, b)
            taps.append(
                ref[da : da + rows, db * ps : db * ps + cols, :].reshape(rows * cols, chan)
            )
    return jnp.concatenate(taps, axis=1)


def silu(v):
    return v * (0.5 * jnp.tanh(0.5 * v) + 0.5)


def make_kernel(lon_n, lat_n, rows, cols, chan, width):
    pr, ps = rows // POOL, cols // POOL
    keys = pr * ps
    heads = width // HEAD_DIM
    hq = heads * ps
    group = chan // HEAD_DIM
    groups = heads // group
    gq = group * ps
    slab_rows = (POOL + 2) * ps
    chips = lon_n // 2
    slot_shift = list(range(0, chips, 2)) + list(range(1, chips, 2))
    split = chips // 2
    halo = [
        (0, 0, 1, 0), (1, 0, -1, 0),
        (0, 1, 1, 1), (1, 1, -1, 1),
        (0, 2, 1, -1), (1, 2, -1, -1),
    ]

    def kernel(
        field, conv_w, wq_h, wk_h, wv_h, qrow, ag_h,
        attended, gout,
        xr, xs, xh, cg, ch, cw, wq, wk, wv, ag,
        cout, ccol, grow, dsl, nall, chosen, ntr, ex, dpr, pt, utb, gall, part, recv,
        stat, joined, colmsg, colhalo, colend, dslrow, dslhalo, pgb, pgcell, pgmid, pgend, pgrow,
        load_sem, send_sem, recv_sem,
    ):
        lon = lax.axis_index("lon")
        lat = lax.axis_index("lat")
        count = itertools.count()

        def at(dlon, dlat):
            return {
                "lon": lax.rem(lon + dlon + lon_n, lon_n),
                "lat": lax.rem(lat + dlat + lat_n, lat_n),
            }

        sibling = {"lon": lon + 1 - 2 * lax.rem(lon, 2), "lat": lat}

        def remote(src, dst, device):
            k = next(count)
            return pltpu.make_async_remote_copy(
                src_ref=src,
                dst_ref=dst,
                send_sem=send_sem.at[k],
                recv_sem=recv_sem.at[k],
                device_id=device,
                device_id_type=MESH,
            )

        def start(copies):
            for c in copies:
                c.start()

        def wait(copies):
            for c in copies:
                c.wait()

        loads = [
            pltpu.make_async_copy(field, xr, load_sem.at[0]),
            pltpu.make_async_copy(conv_w, cw, load_sem.at[1]),
            pltpu.make_async_copy(ag_h.at[0], ag.at[0], load_sem.at[2]),
            pltpu.make_async_copy(wv_h, wv, load_sem.at[3]),
            pltpu.make_async_copy(wq_h, wq, load_sem.at[4]),
            pltpu.make_async_copy(wk_h, wk, load_sem.at[5]),
        ]
        loads[0].start()

        barrier = pltpu.get_barrier_semaphore()
        friends = [(0, -1), (0, 1)] + [(dlon, dlat) for _, _, dlon, dlat in halo]
        friends += [(2 * e, 0) for e in range(1, chips)]
        for dlon, dlat in friends:
            pl.semaphore_signal(barrier, inc=1, device_id=at(dlon, dlat), device_id_type=MESH)
        start(loads[1:])

        def columns(phase):
            mids, ends = [], []
            for side, place, dlon, dlat in halo:
                if place == 0:
                    src, dst = colmsg.at[phase, side], colhalo.at[phase, side]
                    mids.append(remote(src, dst, at(dlon, dlat)))
                else:
                    cell = pl.ds(rows - 1 if place == 1 else 0, 1)
                    src = colmsg.at[phase, side, cell]
                    dst = colend.at[phase, side, place - 1, pl.ds(0, 1)]
                    ends.append(remote(src, dst, at(dlon, dlat)))
            return mids, ends

        prow = lax.broadcasted_iota(jnp.int32, (slab_rows, cols), 0)
        pcol = lax.broadcasted_iota(jnp.int32, (slab_rows, cols), 1)
        spread = jnp.where(
            pcol == lax.rem(prow, ps) * POOL + lax.div(prow, ps) - 1, 1.0, 0.0
        ).astype(BF16)
        mid = pl.ds(ps, cols)

        loads[0].wait()
        for i in (0, rows - 1):
            xs[1 + i] = mm(spread, xr[i]).astype(BF16)
        for i in range(rows):
            colmsg[0, 0, i : i + 1, :] = xr[i, cols - 16 : cols, :].astype(F32)[15:16]
            colmsg[0, 1, i : i + 1, :] = xr[i, 0:16, :].astype(F32)[0:1]
        pl.semaphore_wait(barrier, len(friends))
        field_rows = [
            remote(xs.at[1, mid], xh.at[1, mid], at(0, -1)),
            remote(xs.at[rows, mid], xh.at[0, mid], at(0, 1)),
        ]
        field_cols, field_ends = columns(0)
        grads = remote(ag_h.at[0], ag.at[1], sibling)
        start(field_rows + field_cols + field_ends + [grads])

        xs[0] = jnp.zeros((slab_rows, chan), BF16)
        xs[rows + 1] = jnp.zeros((slab_rows, chan), BF16)
        for i in range(1, rows - 1):
            xs[1 + i] = mm(spread, xr[i]).astype(BF16)
        loads[1].wait()
        cout[...] = mm(windows(xs, rows, cols, ps, False), cw[...].reshape(9 * chan, chan))
        pooled = []
        for p in range(pr):
            lo, hi = max(p * POOL, 1), min((p + 1) * POOL, rows - 1)
            act = silu(cout[lo * cols : hi * cols, :])
            pooled.append(act.reshape((hi - lo) * POOL, ps, chan).sum(axis=0))
        for i in range(rows):
            ccol[0, i : i + 1, :] = cout[i * cols : i * cols + 1, :]
            ccol[1, i : i + 1, :] = cout[(i + 1) * cols - 1 : (i + 1) * cols, :]

        edge = lax.broadcasted_iota(jnp.int32, (ps, chan), 0)
        line = lax.broadcasted_iota(jnp.int32, (rows, chan), 0)

        def column_taps(cells):
            above = jnp.where(line == 0, 0.0, pltpu.roll(cells, 1, 0))
            below = jnp.where(line == rows - 1, 0.0, pltpu.roll(cells, rows - 1, 0))
            return above, cells, below

        def column_terms(left, right, weights, dims):
            none = jnp.zeros((rows, 3 * chan), F32)
            left, right = jnp.concatenate(left, axis=1), jnp.concatenate(right, axis=1)
            lhs = jnp.concatenate(
                [
                    jnp.concatenate([left, none], axis=1),
                    jnp.concatenate([none, right], axis=1),
                ],
                axis=0,
            ).astype(BF16)
            axis = 1 if dims == NT else 0
            y = mm(lhs, jnp.concatenate(weights, axis=axis), dims)
            return y[:rows], y[rows:]

        def row_slabs(ref, k, first_slab, last_slab, left, right):
            lo = pltpu.roll(last_slab, 1, 0)
            hi = pltpu.roll(first_slab, ps - 1, 0)
            ref[k, 0:ps, :] = jnp.where(edge == 0, left, lo).astype(BF16)
            ref[k, slab_rows - ps : slab_rows, :] = jnp.where(edge == ps - 1, right, hi).astype(
                BF16
            )

        hrow = lax.div(lax.broadcasted_iota(jnp.int32, (gq, chan), 0), ps)
        hcol = lax.div(lax.broadcasted_iota(jnp.int32, (gq, chan), 1), HEAD_DIM)
        head_mask = hrow == hcol

        def absorb(x, w_ref, base, scale):
            for g in range(groups):
                x_g = x[:, g * chan : (g + 1) * chan]
                wide = jnp.where(head_mask, jnp.concatenate([x_g] * group, axis=0), 0.0)
                y = mm(wide.astype(BF16), w_ref[:, g * chan : (g + 1) * chan], NT)
                y = y * scale if scale != 1.0 else y
                gall[base + g * gq : base + (g + 1) * gq, :] = y.astype(BF16)

        loads[2].wait()
        loads[3].wait()
        absorb(ag[0].astype(F32), wv, 0, 1.0)

        wait(field_cols)
        fixes = column_terms(
            column_taps(colhalo[0, 0]),
            column_taps(colhalo[0, 1]),
            [cw[a, 0] for a in range(3)] + [cw[a, 2] for a in range(3)],
            NN,
        )
        for side in range(2):
            before = ccol[side]
            after = before + fixes[side]
            ccol[side] = after
            change = silu(after) - silu(before)
            cell = edge == (0, ps - 1)[side]
            for p in range(pr):
                lo, hi = max(p * POOL, 1), min((p + 1) * POOL, rows - 1)
                part_sum = jnp.where((line >= lo) & (line < hi), change, 0.0).sum(
                    axis=0, keepdims=True
                )
                pooled[p] = pooled[p] + jnp.where(cell, part_sum, 0.0)
        for i in range(rows):
            cout[i * cols : i * cols + 1, :] = ccol[0, i : i + 1, :]
            cout[(i + 1) * cols - 1 : (i + 1) * cols, :] = ccol[1, i : i + 1, :]
        wait(field_rows + field_ends)
        for k, pole in ((0, 0), (1, lat_n - 1)):
            there = jnp.where(lat == pole, 0.0, 1.0)
            row_slabs(
                xh,
                k,
                xh[k, ps : 2 * ps, :].astype(F32),
                xh[k, POOL * ps : (POOL + 1) * ps, :].astype(F32),
                colend[0, 0, k, 0:1, :],
                colend[0, 1, k, 0:1, :],
            )
            lhs = jnp.concatenate([xh[k, b * ps : b * ps + cols, :] for b in range(3)], axis=1)
            fix = mm(lhs, cw[2 * k].reshape(3 * chan, chan)) * there
            i = k * (rows - 1)
            v = cout[i * cols : (i + 1) * cols, :] + fix
            cout[i * cols : (i + 1) * cols, :] = v
            p = k * (pr - 1)
            pooled[p] = pooled[p] + silu(v).reshape(POOL, ps, chan).sum(axis=0)
        pooled = jnp.concatenate(pooled, axis=0) * (1.0 / (POOL * POOL))
        centred = pooled - pooled.mean(-1, keepdims=True)
        inv_std = lax.rsqrt((centred * centred).mean(-1, keepdims=True) + NORM_EPS)
        standard = centred * inv_std
        nall[0] = standard.astype(BF16)
        first = qrow[0] == 0
        chosen[0] = jnp.where(first, standard[:ps], standard[ps:]).astype(BF16)

        gathers = [
            remote(nall.at[0], nall.at[k], at(2 * slot_shift[k], 0)) for k in range(1, chips)
        ]
        picks = remote(chosen.at[0], chosen.at[1], sibling)
        start([picks] + gathers[split - 1 :] + gathers[: split - 1])

        loads[4].wait()
        loads[5].wait()
        picks.wait()
        q = mm(chosen[...].reshape(2 * ps, chan), wq[...]).astype(BF16).astype(F32)
        absorb(q[:ps], wk, 2 * hq, HEAD_DIM**-0.5)
        absorb(q[ps:], wk, 3 * hq, HEAD_DIM**-0.5)
        grads.wait()
        absorb(ag[1].astype(F32), wv, hq, 1.0)
        for i in range(rows):
            v = cout[i * cols : (i + 1) * cols, :]
            sig = 0.5 * jnp.tanh(0.5 * v) + 0.5
            d = sig * (1.0 + v * (1.0 - sig)) * (1.0 / (POOL * POOL))
            dsl[i * cols : (i + 1) * cols, :] = d
            colmsg[1, 1, i : i + 1, :] = d[0:1]
            colmsg[1, 0, i : i + 1, :] = d[cols - 1 : cols]
            if i == 0:
                dslrow[0] = d.astype(BF16)
            if i == rows - 1:
                dslrow[1] = d.astype(BF16)
        ident = eye(chan)

        wait(gathers)
        slope_rows = [
            remote(dslrow.at[0], dslhalo.at[1], at(0, -1)),
            remote(dslrow.at[1], dslhalo.at[0], at(0, 1)),
        ]
        slope_cols, slope_ends = columns(1)
        start(slope_rows + slope_cols + slope_ends)
        blk = chan
        nv = nall[...].reshape(chips * keys, chan)
        for h0 in range(0, 2 * hq, blk):
            s = mm(nv, gall[2 * hq + h0 : 2 * hq + h0 + blk, :], NT)
            top = s.max(axis=0, keepdims=True)
            e = jnp.exp(s - top)
            dp = mm(nv, gall[h0 : h0 + blk, :], NT)
            ex[:, h0 : h0 + blk] = e
            dpr[:, h0 : h0 + blk] = dp
            stat[0, 0:1, h0 : h0 + blk] = top
            stat[0, 1:2, h0 : h0 + blk] = e.sum(axis=0, keepdims=True)
            stat[0, 2:3, h0 : h0 + blk] = (e * dp).sum(axis=0, keepdims=True)
        stats = remote(stat.at[0], stat.at[1], sibling)
        stats.start()
        ntr[...] = mm(ident, nv, NT).astype(BF16)
        stats.wait()
        scale = {}
        for h0 in range(0, 2 * hq, blk):
            o0 = (h0 + hq) % (2 * hq)
            top, size, dot = (stat[0, k : k + 1, h0 : h0 + blk] for k in range(3))
            top2, size2, dot2 = (stat[1, k : k + 1, o0 : o0 + blk] for k in range(3))
            peak = jnp.maximum(top, top2)
            f, f2 = jnp.exp(top - peak), jnp.exp(top2 - peak)
            inv = 1.0 / (size * f + size2 * f2)
            scale[h0] = (f * inv, (dot * f + dot2 * f2) * inv)

        scatters = []
        own = None
        for h0 in range(0, 2 * hq, blk):
            prob = ex[:, h0 : h0 + blk] * scale[h0][0]
            pt[:, h0 : h0 + blk] = prob.astype(BF16)
            pt[:, 2 * hq + h0 : 2 * hq + h0 + blk] = (
                prob * (dpr[:, h0 : h0 + blk] - scale[h0][1])
            ).astype(BF16)
        pair = split // 2
        for k0 in (split, 0, split + pair, pair):
            y = mm(pt[k0 * keys : (k0 + pair) * keys, :], gall[...])
            if k0 == 0:
                own = y[:keys]
            part[k0 : k0 + pair] = y.astype(BF16).reshape(pair, keys, chan)
            for k in range(max(k0, 1), k0 + pair):
                scatters.append(remote(part.at[k], recv.at[k], at(-2 * slot_shift[k], 0)))
                scatters[-1].start()

        utb[...] = mm(ntr[...], pt[...]).astype(BF16)
        ident_g = eye(gq)
        mine = None
        for owner in (1, 0):
            outs = []
            qfeat = jnp.zeros((ps, chan), F32)
            for g in range(groups):
                for which in range(2):
                    c0 = (2 * which + owner) * hq + g * gq
                    u = mm(ident_g, utb[:, c0 : c0 + gq], NT).astype(BF16)
                    w = (wv, wk)[which][:, g * chan : (g + 1) * chan]
                    y = jnp.where(head_mask, mm(u, w), 0.0).reshape(group, ps, chan).sum(axis=0)
                    if which == 0:
                        outs.append(y)
                    else:
                        y = (y * HEAD_DIM**-0.5).astype(BF16)
                        qfeat = qfeat + mm(y, wq[:, g * chan : (g + 1) * chan], NT)
            if owner == 1:
                for g in range(groups):
                    joined[0, :, g * chan : (g + 1) * chan] = outs[g]
                joined[0, :, width : width + chan] = qfeat
                joins = remote(joined.at[0], joined.at[1], sibling)
                joins.start()
            else:
                mine = (outs, qfeat)
        joins.wait()
        outs, qfeat = mine
        for g in range(groups):
            cell = slice(g * chan, (g + 1) * chan)
            attended[0, :, cell] = (outs[g] + joined[1, :, cell]).astype(BF16)
        qfeat = qfeat + joined[1, :, width : width + chan]

        zero = jnp.zeros_like(qfeat)
        total = own + jnp.concatenate(
            [jnp.where(first, qfeat, zero), jnp.where(first, zero, qfeat)], axis=0
        )
        wait(slope_rows + slope_cols + slope_ends)
        wait(scatters)
        total = total + recv[1:].astype(F32).sum(axis=0)
        pgrad = inv_std * (
            total
            - total.mean(-1, keepdims=True)
            - standard * (total * standard).mean(-1, keepdims=True)
        )
        pgb[...] = pgrad.astype(BF16).reshape(pr, ps, chan)
        for side in range(2):
            for p in range(pr):
                r = p * ps + (ps - 1, 0)[side]
                pgcell[side * pr + p : side * pr + p + 1, :] = pgrad[r : r + 1]
        pg_rows = [
            remote(pgb.at[0], pgrow.at[1], at(0, -1)),
            remote(pgb.at[pr - 1], pgrow.at[0], at(0, 1)),
        ]
        pg_cols, pg_ends = [], []
        for side, place, dlon, dlat in halo:
            if place == 0:
                src, dst = pgcell.at[pl.ds(side * pr, pr)], pgmid.at[side, pl.ds(0, pr)]
                pg_cols.append(remote(src, dst, at(dlon, dlat)))
            else:
                src = pgcell.at[pl.ds(side * pr + (pr - 1 if place == 1 else 0), 1)]
                dst = pgend.at[side, place - 1, pl.ds(0, 1)]
                pg_ends.append(remote(src, dst, at(dlon, dlat)))
        start(pg_rows + pg_ends + pg_cols)

        cg[0] = jnp.zeros((slab_rows, chan), BF16)
        cg[rows + 1] = jnp.zeros((slab_rows, chan), BF16)
        for i in range(rows):
            p = i // POOL
            pg = pgrad[p * ps : (p + 1) * ps]
            slabs = [
                pg * dsl[i * cols + t * ps : i * cols + (t + 1) * ps, :] for t in range(POOL)
            ]
            for t in range(POOL):
                cg[1 + i, (t + 1) * ps : (t + 2) * ps, :] = slabs[t].astype(BF16)
            row_slabs(cg, 1 + i, slabs[0], slabs[POOL - 1], 0.0, 0.0)
        weights = jnp.concatenate([cw[a, b] for a in range(3) for b in range(3)], axis=1)
        y = mm(windows(cg, rows, cols, ps, True), weights, NT)
        wrow = lax.broadcasted_iota(jnp.int32, (cols, cols), 0)
        wcol = lax.broadcasted_iota(jnp.int32, (cols, cols), 1)
        weave = jnp.where(
            wrow == lax.rem(wcol, ps) * POOL + lax.div(wcol, ps), 1.0, 0.0
        ).astype(BF16)
        grow[0] = y[:cols]
        grow[1] = y[(rows - 1) * cols :]
        for i in range(1, rows - 1):
            gout[i] = mm(weave, y[i * cols : (i + 1) * cols].astype(BF16)).astype(BF16)

        wait(pg_cols)
        halves = []
        for side in range(2):
            cells = jnp.where(line < POOL, pgmid[side, 0:1, :], pgmid[side, 1:2, :])
            halves.append(column_taps(cells * colhalo[1, side])[::-1])
        fixes = column_terms(
            halves[0],
            halves[1],
            [cw[a, 2] for a in range(3)] + [cw[a, 0] for a in range(3)],
            NT,
        )
        tile_row = lax.broadcasted_iota(jnp.int32, (16, chan), 0)
        for i in range(1, rows - 1):
            for side, cut, cell in ((0, slice(0, 16), 0), (1, slice(cols - 16, cols), 15)):
                gout[i, cut, :] = (
                    gout[i, cut, :].astype(F32)
                    + jnp.where(tile_row == cell, fixes[side][i : i + 1], 0.0)
                ).astype(BF16)
        wait(pg_rows + pg_ends)
        for k, pole in ((0, 0), (1, lat_n - 1)):
            there = jnp.where(lat == pole, 0.0, 1.0)
            pg = pgrow[k].astype(F32)
            slope = dslhalo[k].astype(F32)
            slabs = [pg * slope[t * ps : (t + 1) * ps] for t in range(POOL)]
            for t in range(POOL):
                ch[k, (t + 1) * ps : (t + 2) * ps, :] = slabs[t].astype(BF16)
            row_slabs(
                ch,
                k,
                slabs[0],
                slabs[POOL - 1],
                pgend[0, k, 0:1, :] * colend[1, 0, k, 0:1, :],
                pgend[1, k, 0:1, :] * colend[1, 1, k, 0:1, :],
            )
            lhs = jnp.concatenate(
                [ch[k, (2 - b) * ps : (2 - b) * ps + cols, :] for b in range(3)], axis=1
            )
            a = 2 - 2 * k
            y = mm(lhs, jnp.concatenate([cw[a, b] for b in range(3)], axis=1), NT)
            i = k * (rows - 1)
            y = grow[k] + y * there
            first_slab = y[:ps] + jnp.where(edge == 0, fixes[0][i : i + 1], 0.0)
            last_slab = y[cols - ps :] + jnp.where(edge == ps - 1, fixes[1][i : i + 1], 0.0)
            y = jnp.concatenate([first_slab, y[ps : cols - ps], last_slab], axis=0)
            gout[i] = mm(weave, y.astype(BF16)).astype(BF16)

    return kernel


def store_kernel(att, gout, attended, out_grad, sem):
    copies = [
        pltpu.make_async_copy(gout, out_grad, sem.at[0]),
        pltpu.make_async_copy(att, attended, sem.at[1]),
    ]
    for copy in copies:
        copy.start()
    for copy in copies:
        copy.wait()


def solution(mesh):
    lon_n, lat_n = mesh.shape["lon"], mesh.shape["lat"]

    def on_device(field, conv_w, wq, wk, wv, query_rows, attended_grad):
        rows, cols, chan = field.shape
        width = wq.shape[1]
        pr, ps = rows // POOL, cols // POOL
        keys = pr * ps
        chips = lon_n // 2
        hq = (width // HEAD_DIM) * ps
        slab_rows = (POOL + 2) * ps
        any_spec = pl.BlockSpec(memory_space=pl.ANY)
        vmem = pl.BlockSpec(memory_space=pltpu.VMEM)
        att, gout = pl.pallas_call(
            make_kernel(lon_n, lat_n, rows, cols, chan, width),
            out_shape=(
                pltpu.VMEM(attended_grad.shape, BF16),
                pltpu.VMEM(field.shape, BF16),
            ),
            in_specs=[any_spec] * 5 + [vmem, any_spec],
            out_specs=(vmem, vmem),
            scratch_shapes=[
                pltpu.VMEM((rows, cols, chan), BF16),
                pltpu.VMEM((rows + 2, slab_rows, chan), BF16),
                pltpu.VMEM((2, slab_rows, chan), BF16),
                pltpu.VMEM((rows + 2, slab_rows, chan), BF16),
                pltpu.VMEM((2, slab_rows, chan), BF16),
                pltpu.VMEM((3, 3, chan, chan), BF16),
                pltpu.VMEM((chan, width), BF16),
                pltpu.VMEM((chan, width), BF16),
                pltpu.VMEM((chan, width), BF16),
                pltpu.VMEM((2, ps, width), BF16),
                pltpu.VMEM((rows * cols, chan), F32),
                pltpu.VMEM((2, rows, chan), F32),
                pltpu.VMEM((2, cols, chan), F32),
                pltpu.VMEM((rows * cols, chan), F32),
                pltpu.VMEM((chips, keys, chan), BF16),
                pltpu.VMEM((2, ps, chan), BF16),
                pltpu.VMEM((chan, chips * keys), BF16),
                pltpu.VMEM((chips * keys, 2 * hq), F32),
                pltpu.VMEM((chips * keys, 2 * hq), F32),
                pltpu.VMEM((chips * keys, 4 * hq), BF16),
                pltpu.VMEM((chan, 4 * hq), BF16),
                pltpu.VMEM((4 * hq, chan), BF16),
                pltpu.VMEM((chips, keys, chan), BF16),
                pltpu.VMEM((chips, keys, chan), BF16),
                pltpu.VMEM((2, 8, 2 * hq), F32),
                pltpu.VMEM((2, ps, width + chan), F32),
                pltpu.VMEM((2, 2, rows, chan), F32),
                pltpu.VMEM((2, 2, rows, chan), F32),
                pltpu.VMEM((2, 2, 2, 8, chan), F32),
                pltpu.VMEM((2, cols, chan), BF16),
                pltpu.VMEM((2, cols, chan), BF16),
                pltpu.VMEM((pr, ps, chan), BF16),
                pltpu.VMEM((8, chan), F32),
                pltpu.VMEM((2, 8, chan), F32),
                pltpu.VMEM((2, 2, 8, chan), F32),
                pltpu.VMEM((2, ps, chan), BF16),
                pltpu.SemaphoreType.DMA((6,)),
                pltpu.SemaphoreType.DMA((48,)),
                pltpu.SemaphoreType.DMA((48,)),
            ],
            compiler_params=pltpu.CompilerParams(
                collective_id=0, has_side_effects=True, vmem_limit_bytes=55 * 1024 * 1024
            ),
        )(field, conv_w, wq, wk, wv, query_rows, attended_grad)
        return pl.pallas_call(
            store_kernel,
            out_shape=(
                jax.ShapeDtypeStruct(attended_grad.shape, BF16),
                jax.ShapeDtypeStruct(field.shape, BF16),
            ),
            in_specs=[vmem] * 2,
            out_specs=(any_spec, any_spec),
            scratch_shapes=[pltpu.SemaphoreType.DMA((2,))],
            compiler_params=pltpu.CompilerParams(vmem_limit_bytes=4 * 1024 * 1024),
        )(att, gout)

    return jax.shard_map(
        on_device,
        mesh=mesh,
        in_specs=(
            P("lat", "lon", None),
            P(),
            P(),
            P(),
            P(),
            P("lat", "lon", None),
            P("lat", "lon", None),
        ),
        out_specs=(P("lat", "lon", None), P("lat", "lon", None)),
        check_vma=False,
    )
```

```python
import itertools

import jax
import jax.numpy as jnp
from jax import lax
from jax.experimental import pallas as pl
from jax.experimental.pallas import tpu as pltpu
from jax.sharding import PartitionSpec as P

HEAD_DIM = 64
NORM_EPS = 1e-05
POOL = 4
BF16 = jnp.bfloat16
F32 = jnp.float32
MESH = pl.DeviceIdType.MESH

NN = (((1,), (0,)), ((), ()))
NT = (((1,), (1,)), ((), ()))


def mm(a, b, dims=NN):
    return lax.dot_general(a, b, dims, preferred_element_type=F32)


def eye(n):
    rows = lax.broadcasted_iota(jnp.int32, (n, n), 0)
    cols = lax.broadcasted_iota(jnp.int32, (n, n), 1)
    return jnp.where(rows == cols, 1.0, 0.0).astype(BF16)


def windows(ref, rows, cols, ps, flip):
    chan = ref.shape[-1]
    taps = []
    for a in range(3):
        for b in range(3):
            da, db = (2 - a, 2 - b) if flip else (a, b)
            taps.append(
                ref[da : da + rows, db * ps : db * ps + cols, :].reshape(rows * cols, chan)
            )
    return jnp.concatenate(taps, axis=1)


def silu(v):
    return v * (0.5 * jnp.tanh(0.5 * v) + 0.5)


def make_kernel(lon_n, lat_n, rows, cols, chan, width):
    pr, ps = rows // POOL, cols // POOL
    keys = pr * ps
    heads = width // HEAD_DIM
    hq = heads * ps
    group = chan // HEAD_DIM
    groups = heads // group
    gq = group * ps
    slab_rows = (POOL + 2) * ps
    chips = lon_n // 2
    slot_shift = sorted(range(chips), key=lambda e: (e % 2, min(e, chips - e)))
    split = chips // 2
    halo = [
        (0, 0, 1, 0), (1, 0, -1, 0),
        (0, 1, 1, 1), (1, 1, -1, 1),
        (0, 2, 1, -1), (1, 2, -1, -1),
    ]

    def kernel(
        field, conv_w, wq_h, wk_h, wv_h, qrow, ag_h,
        attended, gout,
        xr, xs, xh, cg, cw, wq, wk, wv, ag,
        cout, ccol, grow, dsl, nall, chosen, ntr, ex, dpr, pt, utb, gall, part, recv,
        stat, joined, colmsg, colhalo, colend, dslrow, dslhalo, pgb, pgcell, pgmid, pgend, pgrow,
        load_sem, send_sem, recv_sem,
    ):
        lon = lax.axis_index("lon")
        lat = lax.axis_index("lat")
        count = itertools.count()

        def at(dlon, dlat):
            return {
                "lon": lax.rem(lon + dlon + lon_n, lon_n),
                "lat": lax.rem(lat + dlat + lat_n, lat_n),
            }

        sibling = {"lon": lon + 1 - 2 * lax.rem(lon, 2), "lat": lat}

        def remote(src, dst, device):
            k = next(count)
            return pltpu.make_async_remote_copy(
                src_ref=src,
                dst_ref=dst,
                send_sem=send_sem.at[k],
                recv_sem=recv_sem.at[k],
                device_id=device,
                device_id_type=MESH,
            )

        def start(copies):
            for c in copies:
                c.start()

        def wait(copies):
            for c in copies:
                c.wait()

        loads = [
            pltpu.make_async_copy(field, xr, load_sem.at[0]),
            pltpu.make_async_copy(conv_w, cw, load_sem.at[1]),
            pltpu.make_async_copy(ag_h.at[0], ag.at[0], load_sem.at[2]),
            pltpu.make_async_copy(wv_h, wv, load_sem.at[3]),
            pltpu.make_async_copy(wq_h, wq, load_sem.at[4]),
            pltpu.make_async_copy(wk_h, wk, load_sem.at[5]),
        ]
        loads[0].start()

        barrier = pltpu.get_barrier_semaphore()
        friends = [(0, -1), (0, 1)] + [(dlon, dlat) for _, _, dlon, dlat in halo]
        friends += [(2 * e, 0) for e in range(1, chips)]
        for dlon, dlat in friends:
            pl.semaphore_signal(barrier, inc=1, device_id=at(dlon, dlat), device_id_type=MESH)
        start(loads[1:])

        def columns(phase):
            mids, ends = [], []
            for side, place, dlon, dlat in halo:
                if place == 0:
                    src, dst = colmsg.at[phase, side], colhalo.at[phase, side]
                    mids.append(remote(src, dst, at(dlon, dlat)))
                else:
                    cell = pl.ds(rows - 1 if place == 1 else 0, 1)
                    src = colmsg.at[phase, side, cell]
                    dst = colend.at[phase, side, place - 1, pl.ds(0, 1)]
                    ends.append(remote(src, dst, at(dlon, dlat)))
            return mids, ends

        prow = lax.broadcasted_iota(jnp.int32, (slab_rows, cols), 0)
        pcol = lax.broadcasted_iota(jnp.int32, (slab_rows, cols), 1)
        spread = jnp.where(
            pcol == lax.rem(prow, ps) * POOL + lax.div(prow, ps) - 1, 1.0, 0.0
        ).astype(BF16)
        mid = pl.ds(ps, cols)

        loads[0].wait()
        for i in (0, rows - 1):
            xs[1 + i] = mm(spread, xr[i]).astype(BF16)
        for i in range(rows):
            colmsg[0, 0, i : i + 1, :] = xr[i, cols - 16 : cols, :].astype(F32)[15:16]
            colmsg[0, 1, i : i + 1, :] = xr[i, 0:16, :].astype(F32)[0:1]
        pl.semaphore_wait(barrier, len(friends))
        field_rows = [
            remote(xs.at[1, mid], xh.at[1], at(0, -1)),
            remote(xs.at[rows, mid], xh.at[0], at(0, 1)),
        ]
        field_cols, field_ends = columns(0)
        grads = remote(ag_h.at[0], ag.at[1], sibling)
        start(field_rows + field_cols + field_ends + [grads])

        xs[0] = jnp.zeros((slab_rows, chan), BF16)
        xs[rows + 1] = jnp.zeros((slab_rows, chan), BF16)
        for i in range(1, rows - 1):
            xs[1 + i] = mm(spread, xr[i]).astype(BF16)
        loads[1].wait()
        cout[...] = mm(windows(xs, rows, cols, ps, False), cw[...].reshape(9 * chan, chan))
        pooled = []
        for p in range(pr):
            lo, hi = max(p * POOL, 1), min((p + 1) * POOL, rows - 1)
            act = silu(cout[lo * cols : hi * cols, :])
            pooled.append(act.reshape((hi - lo) * POOL, ps, chan).sum(axis=0))
        for i in range(rows):
            ccol[0, i : i + 1, :] = cout[i * cols : i * cols + 1, :]
            ccol[1, i : i + 1, :] = cout[(i + 1) * cols - 1 : (i + 1) * cols, :]

        edge = lax.broadcasted_iota(jnp.int32, (ps, chan), 0)
        line = lax.broadcasted_iota(jnp.int32, (rows, chan), 0)

        def column_taps(cells):
            above = jnp.where(line == 0, 0.0, pltpu.roll(cells, 1, 0))
            below = jnp.where(line == rows - 1, 0.0, pltpu.roll(cells, rows - 1, 0))
            return above, cells, below

        def column_terms(left, right, weights, dims):
            none = jnp.zeros((rows, 3 * chan), F32)
            left, right = jnp.concatenate(left, axis=1), jnp.concatenate(right, axis=1)
            lhs = jnp.concatenate(
                [
                    jnp.concatenate([left, none], axis=1),
                    jnp.concatenate([none, right], axis=1),
                ],
                axis=0,
            ).astype(BF16)
            axis = 1 if dims == NT else 0
            y = mm(lhs, jnp.concatenate(weights, axis=axis), dims)
            return y[:rows], y[rows:]

        def padded(slabs, left, right):
            lo = jnp.where(edge == 0, left, pltpu.roll(slabs[POOL - 1], 1, 0))
            hi = jnp.where(edge == ps - 1, right, pltpu.roll(slabs[0], ps - 1, 0))
            return [slab.astype(BF16) for slab in [lo, *slabs, hi]]

        def row_windows(slabs, shifts):
            return jnp.concatenate(
                [jnp.concatenate(slabs[b : b + POOL], axis=0) for b in shifts], axis=1
            )

        hrow = lax.div(lax.broadcasted_iota(jnp.int32, (gq, chan), 0), ps)
        hcol = lax.div(lax.broadcasted_iota(jnp.int32, (gq, chan), 1), HEAD_DIM)
        head_mask = hrow == hcol

        def absorb(x, w_ref, base, scale):
            for g in range(groups):
                x_g = x[:, g * chan : (g + 1) * chan]
                wide = jnp.where(head_mask, jnp.concatenate([x_g] * group, axis=0), 0.0)
                y = mm(wide.astype(BF16), w_ref[:, g * chan : (g + 1) * chan], NT)
                y = y * scale if scale != 1.0 else y
                gall[base + g * gq : base + (g + 1) * gq, :] = y.astype(BF16)

        loads[2].wait()
        loads[3].wait()
        absorb(ag[0].astype(F32), wv, 0, 1.0)

        wait(field_cols)
        fixes = column_terms(
            column_taps(colhalo[0, 0]),
            column_taps(colhalo[0, 1]),
            [cw[a, 0] for a in range(3)] + [cw[a, 2] for a in range(3)],
            NN,
        )
        for side in range(2):
            before = ccol[side]
            after = before + fixes[side]
            ccol[side] = after
            change = silu(after) - silu(before)
            cell = edge == (0, ps - 1)[side]
            for p in range(pr):
                lo, hi = max(p * POOL, 1), min((p + 1) * POOL, rows - 1)
                part_sum = jnp.where((line >= lo) & (line < hi), change, 0.0).sum(
                    axis=0, keepdims=True
                )
                pooled[p] = pooled[p] + jnp.where(cell, part_sum, 0.0)
        for i in range(rows):
            cout[i * cols : i * cols + 1, :] = ccol[0, i : i + 1, :]
            cout[(i + 1) * cols - 1 : (i + 1) * cols, :] = ccol[1, i : i + 1, :]
        wait(field_rows + field_ends)
        poles = [jnp.where(lat == pole, 0.0, 1.0) for pole in (0, lat_n - 1)]
        lhs = []
        for k in range(2):
            slabs = [xh[k, t * ps : (t + 1) * ps, :].astype(F32) for t in range(POOL)]
            slabs = padded(slabs, colend[0, 0, k, 0:1, :], colend[0, 1, k, 0:1, :])
            lhs.append(row_windows(slabs, range(3)))
        fix = [mm(lhs[k], cw[2 * k].reshape(3 * chan, chan)) * poles[k] for k in range(2)]
        for k in range(2):
            i = k * (rows - 1)
            v = cout[i * cols : (i + 1) * cols, :] + fix[k]
            cout[i * cols : (i + 1) * cols, :] = v
            p = k * (pr - 1)
            pooled[p] = pooled[p] + silu(v).reshape(POOL, ps, chan).sum(axis=0)
        pooled = jnp.concatenate(pooled, axis=0) * (1.0 / (POOL * POOL))
        centred = pooled - pooled.mean(-1, keepdims=True)
        inv_std = lax.rsqrt((centred * centred).mean(-1, keepdims=True) + NORM_EPS)
        standard = centred * inv_std
        nall[0] = standard.astype(BF16)
        first = qrow[0] == 0
        chosen[0] = jnp.where(first, standard[:ps], standard[ps:]).astype(BF16)

        gathers = [
            remote(nall.at[0], nall.at[k], at(2 * slot_shift[k], 0)) for k in range(1, chips)
        ]
        picks = remote(chosen.at[0], chosen.at[1], sibling)
        start([picks] + gathers[: split - 2 : -1] + gathers[split - 2 :: -1])

        loads[4].wait()
        loads[5].wait()
        picks.wait()
        q = mm(chosen[...].reshape(2 * ps, chan), wq[...]).astype(BF16).astype(F32)
        absorb(q[:ps], wk, 2 * hq, HEAD_DIM**-0.5)
        absorb(q[ps:], wk, 3 * hq, HEAD_DIM**-0.5)
        grads.wait()
        absorb(ag[1].astype(F32), wv, hq, 1.0)
        for i in range(rows):
            v = cout[i * cols : (i + 1) * cols, :]
            sig = 0.5 * jnp.tanh(0.5 * v) + 0.5
            d = sig * (1.0 + v * (1.0 - sig)) * (1.0 / (POOL * POOL))
            dsl[i * cols : (i + 1) * cols, :] = d
            colmsg[1, 1, i : i + 1, :] = d[0:1]
            colmsg[1, 0, i : i + 1, :] = d[cols - 1 : cols]
            if i == 0:
                dslrow[0] = d.astype(BF16)
            if i == rows - 1:
                dslrow[1] = d.astype(BF16)
        ident = eye(chan)

        wait(gathers)
        slope_rows = [
            remote(dslrow.at[0], dslhalo.at[1], at(0, -1)),
            remote(dslrow.at[1], dslhalo.at[0], at(0, 1)),
        ]
        slope_cols, slope_ends = columns(1)
        start(slope_rows + slope_cols + slope_ends)
        blk = chan
        nv = nall[...].reshape(chips * keys, chan)
        for h0 in range(0, 2 * hq, blk):
            s = mm(nv, gall[2 * hq + h0 : 2 * hq + h0 + blk, :], NT)
            top = s.max(axis=0, keepdims=True)
            e = jnp.exp(s - top)
            dp = mm(nv, gall[h0 : h0 + blk, :], NT)
            ex[:, h0 : h0 + blk] = e
            dpr[:, h0 : h0 + blk] = dp
            stat[0, 0:1, h0 : h0 + blk] = top
            stat[0, 1:2, h0 : h0 + blk] = e.sum(axis=0, keepdims=True)
            stat[0, 2:3, h0 : h0 + blk] = (e * dp).sum(axis=0, keepdims=True)
        stats = remote(stat.at[0], stat.at[1], sibling)
        stats.start()
        ntr[...] = mm(ident, nv, NT).astype(BF16)
        stats.wait()
        scale = {}
        for h0 in range(0, 2 * hq, blk):
            o0 = (h0 + hq) % (2 * hq)
            top, size, dot = (stat[0, k : k + 1, h0 : h0 + blk] for k in range(3))
            top2, size2, dot2 = (stat[1, k : k + 1, o0 : o0 + blk] for k in range(3))
            peak = jnp.maximum(top, top2)
            f, f2 = jnp.exp(top - peak), jnp.exp(top2 - peak)
            inv = 1.0 / (size * f + size2 * f2)
            scale[h0] = (f * inv, (dot * f + dot2 * f2) * inv)

        scatters = []
        own = None
        for h0 in range(0, 2 * hq, blk):
            prob = ex[:, h0 : h0 + blk] * scale[h0][0]
            pt[:, h0 : h0 + blk] = prob.astype(BF16)
            pt[:, 2 * hq + h0 : 2 * hq + h0 + blk] = (
                prob * (dpr[:, h0 : h0 + blk] - scale[h0][1])
            ).astype(BF16)
        pair = split // 2
        for k0 in (split + pair, pair, split, 0):
            y = mm(pt[k0 * keys : (k0 + pair) * keys, :], gall[...])
            if k0 == 0:
                own = y[:keys]
            part[k0 : k0 + pair] = y.astype(BF16).reshape(pair, keys, chan)
            for k in range(max(k0, 1), k0 + pair):
                scatters.append(remote(part.at[k], recv.at[k], at(-2 * slot_shift[k], 0)))
                scatters[-1].start()

        utb[...] = mm(ntr[...], pt[...]).astype(BF16)
        ident_g = eye(gq)
        mine = None
        for owner in (1, 0):
            outs = []
            qfeat = jnp.zeros((ps, chan), F32)
            for g in range(groups):
                for which in range(2):
                    c0 = (2 * which + owner) * hq + g * gq
                    u = mm(ident_g, utb[:, c0 : c0 + gq], NT).astype(BF16)
                    w = (wv, wk)[which][:, g * chan : (g + 1) * chan]
                    y = jnp.where(head_mask, mm(u, w), 0.0).reshape(group, ps, chan).sum(axis=0)
                    if which == 0:
                        outs.append(y)
                    else:
                        y = (y * HEAD_DIM**-0.5).astype(BF16)
                        qfeat = qfeat + mm(y, wq[:, g * chan : (g + 1) * chan], NT)
            if owner == 1:
                for g in range(groups):
                    joined[0, :, g * chan : (g + 1) * chan] = outs[g]
                joined[0, :, width : width + chan] = qfeat
                joins = remote(joined.at[0], joined.at[1], sibling)
                joins.start()
            else:
                mine = (outs, qfeat)
        joins.wait()
        outs, qfeat = mine
        for g in range(groups):
            cell = slice(g * chan, (g + 1) * chan)
            attended[0, :, cell] = (outs[g] + joined[1, :, cell]).astype(BF16)
        qfeat = qfeat + joined[1, :, width : width + chan]

        zero = jnp.zeros_like(qfeat)
        total = own + jnp.concatenate(
            [jnp.where(first, qfeat, zero), jnp.where(first, zero, qfeat)], axis=0
        )
        wait(slope_rows + slope_cols + slope_ends)
        wait(scatters)
        total = total + recv[1:].astype(F32).sum(axis=0)
        pgrad = inv_std * (
            total
            - total.mean(-1, keepdims=True)
            - standard * (total * standard).mean(-1, keepdims=True)
        )
        pgb[...] = pgrad.astype(BF16).reshape(pr, ps, chan)
        for side in range(2):
            for p in range(pr):
                r = p * ps + (ps - 1, 0)[side]
                pgcell[side * pr + p : side * pr + p + 1, :] = pgrad[r : r + 1]
        pg_rows = [
            remote(pgb.at[0], pgrow.at[1], at(0, -1)),
            remote(pgb.at[pr - 1], pgrow.at[0], at(0, 1)),
        ]
        pg_cols, pg_ends = [], []
        for side, place, dlon, dlat in halo:
            if place == 0:
                src, dst = pgcell.at[pl.ds(side * pr, pr)], pgmid.at[side, pl.ds(0, pr)]
                pg_cols.append(remote(src, dst, at(dlon, dlat)))
            else:
                src = pgcell.at[pl.ds(side * pr + (pr - 1 if place == 1 else 0), 1)]
                dst = pgend.at[side, place - 1, pl.ds(0, 1)]
                pg_ends.append(remote(src, dst, at(dlon, dlat)))
        start(pg_rows + pg_ends + pg_cols)

        cg[0] = jnp.zeros((slab_rows, chan), BF16)
        cg[rows + 1] = jnp.zeros((slab_rows, chan), BF16)
        for i in range(rows):
            p = i // POOL
            pg = pgrad[p * ps : (p + 1) * ps]
            slabs = [
                pg * dsl[i * cols + t * ps : i * cols + (t + 1) * ps, :] for t in range(POOL)
            ]
            for t, slab in enumerate(padded(slabs, 0.0, 0.0)):
                cg[1 + i, t * ps : (t + 1) * ps, :] = slab
        weights = jnp.concatenate([cw[a, b] for a in range(3) for b in range(3)], axis=1)
        y = mm(windows(cg, rows, cols, ps, True), weights, NT)
        wrow = lax.broadcasted_iota(jnp.int32, (cols, cols), 0)
        wcol = lax.broadcasted_iota(jnp.int32, (cols, cols), 1)
        weave = jnp.where(
            wrow == lax.rem(wcol, ps) * POOL + lax.div(wcol, ps), 1.0, 0.0
        ).astype(BF16)
        grow[0] = y[:cols]
        grow[1] = y[(rows - 1) * cols :]
        for i in range(1, rows - 1):
            gout[i] = mm(weave, y[i * cols : (i + 1) * cols].astype(BF16)).astype(BF16)

        wait(pg_cols)
        halves = []
        for side in range(2):
            cells = jnp.where(line < POOL, pgmid[side, 0:1, :], pgmid[side, 1:2, :])
            halves.append(column_taps(cells * colhalo[1, side])[::-1])
        fixes = column_terms(
            halves[0],
            halves[1],
            [cw[a, 2] for a in range(3)] + [cw[a, 0] for a in range(3)],
            NT,
        )
        tile_row = lax.broadcasted_iota(jnp.int32, (16, chan), 0)
        for k in range(2):
            i = k * (rows - 1)
            grow[k, 0:ps, :] = grow[k, 0:ps, :] + jnp.where(edge == 0, fixes[0][i : i + 1], 0.0)
            grow[k, cols - ps : cols, :] = grow[k, cols - ps : cols, :] + jnp.where(
                edge == ps - 1, fixes[1][i : i + 1], 0.0
            )
        for i in range(1, rows - 1):
            for side, cut, cell in ((0, slice(0, 16), 0), (1, slice(cols - 16, cols), 15)):
                gout[i, cut, :] = (
                    gout[i, cut, :].astype(F32)
                    + jnp.where(tile_row == cell, fixes[side][i : i + 1], 0.0)
                ).astype(BF16)
        wait(pg_rows + pg_ends)
        lhs = []
        for k in range(2):
            pg = pgrow[k].astype(F32)
            slope = dslhalo[k].astype(F32)
            slabs = [pg * slope[t * ps : (t + 1) * ps] for t in range(POOL)]
            slabs = padded(
                slabs,
                pgend[0, k, 0:1, :] * colend[1, 0, k, 0:1, :],
                pgend[1, k, 0:1, :] * colend[1, 1, k, 0:1, :],
            )
            lhs.append(row_windows(slabs, (2, 1, 0)))
        y = [
            mm(lhs[k], jnp.concatenate([cw[2 - 2 * k, b] for b in range(3)], axis=1), NT)
            for k in range(2)
        ]
        for k in range(2):
            out = grow[k] + y[k] * poles[k]
            gout[k * (rows - 1)] = mm(weave, out.astype(BF16)).astype(BF16)

    return kernel


def store_kernel(att, gout, attended, out_grad, sem):
    copies = [
        pltpu.make_async_copy(gout, out_grad, sem.at[0]),
        pltpu.make_async_copy(att, attended, sem.at[1]),
    ]
    for copy in copies:
        copy.start()
    for copy in copies:
        copy.wait()


def solution(mesh):
    lon_n, lat_n = mesh.shape["lon"], mesh.shape["lat"]

    def on_device(field, conv_w, wq, wk, wv, query_rows, attended_grad):
        rows, cols, chan = field.shape
        width = wq.shape[1]
        pr, ps = rows // POOL, cols // POOL
        keys = pr * ps
        chips = lon_n // 2
        hq = (width // HEAD_DIM) * ps
        slab_rows = (POOL + 2) * ps
        any_spec = pl.BlockSpec(memory_space=pl.ANY)
        vmem = pl.BlockSpec(memory_space=pltpu.VMEM)
        att, gout = pl.pallas_call(
            make_kernel(lon_n, lat_n, rows, cols, chan, width),
            out_shape=(
                pltpu.VMEM(attended_grad.shape, BF16),
                pltpu.VMEM(field.shape, BF16),
            ),
            in_specs=[any_spec] * 5 + [vmem, any_spec],
            out_specs=(vmem, vmem),
            scratch_shapes=[
                pltpu.VMEM((rows, cols, chan), BF16),
                pltpu.VMEM((rows + 2, slab_rows, chan), BF16),
                pltpu.VMEM((2, cols, chan), BF16),
                pltpu.VMEM((rows + 2, slab_rows, chan), BF16),
                pltpu.VMEM((3, 3, chan, chan), BF16),
                pltpu.VMEM((chan, width), BF16),
                pltpu.VMEM((chan, width), BF16),
                pltpu.VMEM((chan, width), BF16),
                pltpu.VMEM((2, ps, width), BF16),
                pltpu.VMEM((rows * cols, chan), F32),
                pltpu.VMEM((2, rows, chan), F32),
                pltpu.VMEM((2, cols, chan), F32),
                pltpu.VMEM((rows * cols, chan), F32),
                pltpu.VMEM((chips, keys, chan), BF16),
                pltpu.VMEM((2, ps, chan), BF16),
                pltpu.VMEM((chan, chips * keys), BF16),
                pltpu.VMEM((chips * keys, 2 * hq), F32),
                pltpu.VMEM((chips * keys, 2 * hq), F32),
                pltpu.VMEM((chips * keys, 4 * hq), BF16),
                pltpu.VMEM((chan, 4 * hq), BF16),
                pltpu.VMEM((4 * hq, chan), BF16),
                pltpu.VMEM((chips, keys, chan), BF16),
                pltpu.VMEM((chips, keys, chan), BF16),
                pltpu.VMEM((2, 8, 2 * hq), F32),
                pltpu.VMEM((2, ps, width + chan), F32),
                pltpu.VMEM((2, 2, rows, chan), F32),
                pltpu.VMEM((2, 2, rows, chan), F32),
                pltpu.VMEM((2, 2, 2, 8, chan), F32),
                pltpu.VMEM((2, cols, chan), BF16),
                pltpu.VMEM((2, cols, chan), BF16),
                pltpu.VMEM((pr, ps, chan), BF16),
                pltpu.VMEM((8, chan), F32),
                pltpu.VMEM((2, 8, chan), F32),
                pltpu.VMEM((2, 2, 8, chan), F32),
                pltpu.VMEM((2, ps, chan), BF16),
                pltpu.SemaphoreType.DMA((6,)),
                pltpu.SemaphoreType.DMA((48,)),
                pltpu.SemaphoreType.DMA((48,)),
            ],
            compiler_params=pltpu.CompilerParams(
                collective_id=0, has_side_effects=True, vmem_limit_bytes=55 * 1024 * 1024
            ),
        )(field, conv_w, wq, wk, wv, query_rows, attended_grad)
        return pl.pallas_call(
            store_kernel,
            out_shape=(
                jax.ShapeDtypeStruct(attended_grad.shape, BF16),
                jax.ShapeDtypeStruct(field.shape, BF16),
            ),
            in_specs=[vmem] * 2,
            out_specs=(any_spec, any_spec),
            scratch_shapes=[pltpu.SemaphoreType.DMA((2,))],
            compiler_params=pltpu.CompilerParams(vmem_limit_bytes=4 * 1024 * 1024),
        )(att, gout)

    return jax.shard_map(
        on_device,
        mesh=mesh,
        in_specs=(
            P("lat", "lon", None),
            P(),
            P(),
            P(),
            P(),
            P("lat", "lon", None),
            P("lat", "lon", None),
        ),
        out_specs=(P("lat", "lon", None), P("lat", "lon", None)),
        check_vma=False,
    )
```

```python
import itertools

import jax
import jax.numpy as jnp
from jax import lax
from jax.experimental import pallas as pl
from jax.experimental.pallas import tpu as pltpu
from jax.sharding import PartitionSpec as P

HEAD_DIM = 64
NORM_EPS = 1e-05
POOL = 4
BF16 = jnp.bfloat16
F32 = jnp.float32
MESH = pl.DeviceIdType.MESH

NN = (((1,), (0,)), ((), ()))
NT = (((1,), (1,)), ((), ()))


def mm(a, b, dims=NN):
    return lax.dot_general(a, b, dims, preferred_element_type=F32)


def eye(n):
    rows = lax.broadcasted_iota(jnp.int32, (n, n), 0)
    cols = lax.broadcasted_iota(jnp.int32, (n, n), 1)
    return jnp.where(rows == cols, 1.0, 0.0).astype(BF16)


def windows(ref, rows, cols, ps, flip):
    chan = ref.shape[-1]
    taps = []
    for a in range(3):
        for b in range(3):
            da, db = (2 - a, 2 - b) if flip else (a, b)
            taps.append(
                ref[da : da + rows, db * ps : db * ps + cols, :].reshape(rows * cols, chan)
            )
    return jnp.concatenate(taps, axis=1)


def silu(v):
    return v * (0.5 * jnp.tanh(0.5 * v) + 0.5)


def make_kernel(lon_n, lat_n, rows, cols, chan, width):
    pr, ps = rows // POOL, cols // POOL
    keys = pr * ps
    heads = width // HEAD_DIM
    hq = heads * ps
    group = chan // HEAD_DIM
    groups = heads // group
    gq = group * ps
    slab_rows = (POOL + 2) * ps
    chips = lon_n // 2
    slot_shift = sorted(range(chips), key=lambda e: (e % 2, min(e, chips - e)))
    split = chips // 2
    halo = [
        (0, 0, 1, 0), (1, 0, -1, 0),
        (0, 1, 1, 1), (1, 1, -1, 1),
        (0, 2, 1, -1), (1, 2, -1, -1),
    ]

    def kernel(
        field, conv_w, wq_h, wk_h, wv_h, qrow, ag_h,
        attended, gout,
        xr, xs, xh, cg, cw, wq, wk, wv, ag,
        cout, ccol, grow, dsl, nall, chosen, ntr, ex, dpr, pt, utb, gall, part, recv,
        stat, joined, colmsg, colhalo, colend, dslrow, dslhalo, pgb, pgcell, pgmid, pgend, pgrow,
        load_sem, send_sem, recv_sem,
    ):
        lon = lax.axis_index("lon")
        lat = lax.axis_index("lat")
        count = itertools.count()

        def at(dlon, dlat):
            return {
                "lon": lax.rem(lon + dlon + lon_n, lon_n),
                "lat": lax.rem(lat + dlat + lat_n, lat_n),
            }

        sibling = {"lon": lon + 1 - 2 * lax.rem(lon, 2), "lat": lat}

        def remote(src, dst, device):
            k = next(count)
            return pltpu.make_async_remote_copy(
                src_ref=src,
                dst_ref=dst,
                send_sem=send_sem.at[k],
                recv_sem=recv_sem.at[k],
                device_id=device,
                device_id_type=MESH,
            )

        def start(copies):
            for c in copies:
                c.start()

        def wait(copies):
            for c in copies:
                c.wait()

        loads = [
            pltpu.make_async_copy(field, xr, load_sem.at[0]),
            pltpu.make_async_copy(conv_w, cw, load_sem.at[1]),
            pltpu.make_async_copy(ag_h.at[0], ag.at[0], load_sem.at[2]),
            pltpu.make_async_copy(wv_h, wv, load_sem.at[3]),
            pltpu.make_async_copy(wq_h, wq, load_sem.at[4]),
            pltpu.make_async_copy(wk_h, wk, load_sem.at[5]),
        ]
        loads[0].start()

        barrier = pltpu.get_barrier_semaphore()
        friends = [(0, -1), (0, 1)] + [(dlon, dlat) for _, _, dlon, dlat in halo]
        friends += [(2 * e, 0) for e in range(1, chips)]
        for dlon, dlat in friends:
            pl.semaphore_signal(barrier, inc=1, device_id=at(dlon, dlat), device_id_type=MESH)
        start(loads[1:])

        def columns(phase):
            mids, ends = [], []
            for side, place, dlon, dlat in halo:
                if place == 0:
                    src, dst = colmsg.at[phase, side], colhalo.at[phase, side]
                    mids.append(remote(src, dst, at(dlon, dlat)))
                else:
                    cell = pl.ds(rows - 1 if place == 1 else 0, 1)
                    src = colmsg.at[phase, side, cell]
                    dst = colend.at[phase, side, place - 1, pl.ds(0, 1)]
                    ends.append(remote(src, dst, at(dlon, dlat)))
            return mids, ends

        prow = lax.broadcasted_iota(jnp.int32, (slab_rows, cols), 0)
        pcol = lax.broadcasted_iota(jnp.int32, (slab_rows, cols), 1)
        spread = jnp.where(
            pcol == lax.rem(prow, ps) * POOL + lax.div(prow, ps) - 1, 1.0, 0.0
        ).astype(BF16)
        mid = pl.ds(ps, cols)

        loads[0].wait()
        for i in (0, rows - 1):
            xs[1 + i] = mm(spread, xr[i]).astype(BF16)
        for i in range(rows):
            colmsg[0, 0, i : i + 1, :] = xr[i, cols - 16 : cols, :].astype(F32)[15:16]
            colmsg[0, 1, i : i + 1, :] = xr[i, 0:16, :].astype(F32)[0:1]
        pl.semaphore_wait(barrier, len(friends))
        field_rows = [
            remote(xs.at[1, mid], xh.at[1], at(0, -1)),
            remote(xs.at[rows, mid], xh.at[0], at(0, 1)),
        ]
        field_cols, field_ends = columns(0)
        grads = remote(ag_h.at[0], ag.at[1], sibling)
        start(field_ends + field_rows + field_cols)

        xs[0] = jnp.zeros((slab_rows, chan), BF16)
        xs[rows + 1] = jnp.zeros((slab_rows, chan), BF16)
        for i in range(1, rows - 1):
            xs[1 + i] = mm(spread, xr[i]).astype(BF16)
        loads[1].wait()
        cout[...] = mm(windows(xs, rows, cols, ps, False), cw[...].reshape(9 * chan, chan))
        pooled = []
        for p in range(pr):
            lo, hi = max(p * POOL, 1), min((p + 1) * POOL, rows - 1)
            act = silu(cout[lo * cols : hi * cols, :])
            pooled.append(act.reshape((hi - lo) * POOL, ps, chan).sum(axis=0))
        for i in range(rows):
            ccol[0, i : i + 1, :] = cout[i * cols : i * cols + 1, :]
            ccol[1, i : i + 1, :] = cout[(i + 1) * cols - 1 : (i + 1) * cols, :]

        edge = lax.broadcasted_iota(jnp.int32, (ps, chan), 0)
        line = lax.broadcasted_iota(jnp.int32, (rows, chan), 0)

        def column_taps(cells):
            above = jnp.where(line == 0, 0.0, pltpu.roll(cells, 1, 0))
            below = jnp.where(line == rows - 1, 0.0, pltpu.roll(cells, rows - 1, 0))
            return above, cells, below

        def column_terms(left, right, weights, dims):
            none = jnp.zeros((rows, 3 * chan), F32)
            left, right = jnp.concatenate(left, axis=1), jnp.concatenate(right, axis=1)
            lhs = jnp.concatenate(
                [
                    jnp.concatenate([left, none], axis=1),
                    jnp.concatenate([none, right], axis=1),
                ],
                axis=0,
            ).astype(BF16)
            axis = 1 if dims == NT else 0
            y = mm(lhs, jnp.concatenate(weights, axis=axis), dims)
            return y[:rows], y[rows:]

        def padded(slabs, left, right):
            lo = jnp.where(edge == 0, left, pltpu.roll(slabs[POOL - 1], 1, 0))
            hi = jnp.where(edge == ps - 1, right, pltpu.roll(slabs[0], ps - 1, 0))
            return [slab.astype(BF16) for slab in [lo, *slabs, hi]]

        def row_windows(slabs, shifts):
            return jnp.concatenate(
                [jnp.concatenate(slabs[b : b + POOL], axis=0) for b in shifts], axis=1
            )

        hrow = lax.div(lax.broadcasted_iota(jnp.int32, (gq, chan), 0), ps)
        hcol = lax.div(lax.broadcasted_iota(jnp.int32, (gq, chan), 1), HEAD_DIM)
        head_mask = hrow == hcol

        def absorb(x, w_ref, base, scale):
            for g in range(groups):
                x_g = x[:, g * chan : (g + 1) * chan]
                wide = jnp.where(head_mask, jnp.concatenate([x_g] * group, axis=0), 0.0)
                y = mm(wide.astype(BF16), w_ref[:, g * chan : (g + 1) * chan], NT)
                y = y * scale if scale != 1.0 else y
                gall[base + g * gq : base + (g + 1) * gq, :] = y.astype(BF16)

        loads[2].wait()
        loads[3].wait()
        absorb(ag[0].astype(F32), wv, 0, 1.0)

        wait(field_cols)
        fixes = column_terms(
            column_taps(colhalo[0, 0]),
            column_taps(colhalo[0, 1]),
            [cw[a, 0] for a in range(3)] + [cw[a, 2] for a in range(3)],
            NN,
        )
        for side in range(2):
            before = ccol[side]
            after = before + fixes[side]
            ccol[side] = after
            change = silu(after) - silu(before)
            cell = edge == (0, ps - 1)[side]
            for p in range(pr):
                lo, hi = max(p * POOL, 1), min((p + 1) * POOL, rows - 1)
                part_sum = jnp.where((line >= lo) & (line < hi), change, 0.0).sum(
                    axis=0, keepdims=True
                )
                pooled[p] = pooled[p] + jnp.where(cell, part_sum, 0.0)
        for i in range(rows):
            cout[i * cols : i * cols + 1, :] = ccol[0, i : i + 1, :]
            cout[(i + 1) * cols - 1 : (i + 1) * cols, :] = ccol[1, i : i + 1, :]
        grads.start()
        wait(field_rows + field_ends)
        poles = [jnp.where(lat == pole, 0.0, 1.0) for pole in (0, lat_n - 1)]
        lhs = []
        for k in range(2):
            slabs = [xh[k, t * ps : (t + 1) * ps, :].astype(F32) for t in range(POOL)]
            slabs = padded(slabs, colend[0, 0, k, 0:1, :], colend[0, 1, k, 0:1, :])
            lhs.append(row_windows(slabs, range(3)))
        fix = [mm(lhs[k], cw[2 * k].reshape(3 * chan, chan)) * poles[k] for k in range(2)]
        for k in range(2):
            i = k * (rows - 1)
            v = cout[i * cols : (i + 1) * cols, :] + fix[k]
            cout[i * cols : (i + 1) * cols, :] = v
            p = k * (pr - 1)
            pooled[p] = pooled[p] + silu(v).reshape(POOL, ps, chan).sum(axis=0)
        pooled = jnp.concatenate(pooled, axis=0) * (1.0 / (POOL * POOL))
        centred = pooled - pooled.mean(-1, keepdims=True)
        inv_std = lax.rsqrt((centred * centred).mean(-1, keepdims=True) + NORM_EPS)
        standard = centred * inv_std
        nall[0] = standard.astype(BF16)
        first = qrow[0] == 0
        chosen[0] = jnp.where(first, standard[:ps], standard[ps:]).astype(BF16)

        gathers = [
            remote(nall.at[0], nall.at[k], at(2 * slot_shift[k], 0)) for k in range(1, chips)
        ]
        picks = remote(chosen.at[0], chosen.at[1], sibling)
        start([picks] + gathers[: split - 2 : -1] + gathers[split - 2 :: -1])

        loads[4].wait()
        loads[5].wait()
        picks.wait()
        q = mm(chosen[...].reshape(2 * ps, chan), wq[...]).astype(BF16).astype(F32)
        absorb(q[:ps], wk, 2 * hq, HEAD_DIM**-0.5)
        absorb(q[ps:], wk, 3 * hq, HEAD_DIM**-0.5)
        grads.wait()
        absorb(ag[1].astype(F32), wv, hq, 1.0)
        for i in range(rows):
            v = cout[i * cols : (i + 1) * cols, :]
            sig = 0.5 * jnp.tanh(0.5 * v) + 0.5
            d = sig * (1.0 + v * (1.0 - sig)) * (1.0 / (POOL * POOL))
            dsl[i * cols : (i + 1) * cols, :] = d
            colmsg[1, 1, i : i + 1, :] = d[0:1]
            colmsg[1, 0, i : i + 1, :] = d[cols - 1 : cols]
            if i == 0:
                dslrow[0] = d.astype(BF16)
            if i == rows - 1:
                dslrow[1] = d.astype(BF16)
        ident = eye(chan)

        wait(gathers)
        slope_rows = [
            remote(dslrow.at[0], dslhalo.at[1], at(0, -1)),
            remote(dslrow.at[1], dslhalo.at[0], at(0, 1)),
        ]
        slope_cols, slope_ends = columns(1)
        start(slope_rows + slope_cols + slope_ends)
        blk = chan
        nv = nall[...].reshape(chips * keys, chan)
        for h0 in range(0, 2 * hq, blk):
            s = mm(nv, gall[2 * hq + h0 : 2 * hq + h0 + blk, :], NT)
            top = s.max(axis=0, keepdims=True)
            e = jnp.exp(s - top)
            dp = mm(nv, gall[h0 : h0 + blk, :], NT)
            ex[:, h0 : h0 + blk] = e
            dpr[:, h0 : h0 + blk] = dp
            stat[0, 0:1, h0 : h0 + blk] = top
            stat[0, 1:2, h0 : h0 + blk] = e.sum(axis=0, keepdims=True)
            stat[0, 2:3, h0 : h0 + blk] = (e * dp).sum(axis=0, keepdims=True)
        stats = remote(stat.at[0], stat.at[1], sibling)
        stats.start()
        ntr[...] = mm(ident, nv, NT).astype(BF16)
        stats.wait()
        scale = {}
        for h0 in range(0, 2 * hq, blk):
            o0 = (h0 + hq) % (2 * hq)
            top, size, dot = (stat[0, k : k + 1, h0 : h0 + blk] for k in range(3))
            top2, size2, dot2 = (stat[1, k : k + 1, o0 : o0 + blk] for k in range(3))
            peak = jnp.maximum(top, top2)
            f, f2 = jnp.exp(top - peak), jnp.exp(top2 - peak)
            inv = 1.0 / (size * f + size2 * f2)
            scale[h0] = (f * inv, (dot * f + dot2 * f2) * inv)

        scatters = []
        own = None
        for h0 in range(0, 2 * hq, blk):
            prob = ex[:, h0 : h0 + blk] * scale[h0][0]
            pt[:, h0 : h0 + blk] = prob.astype(BF16)
            pt[:, 2 * hq + h0 : 2 * hq + h0 + blk] = (
                prob * (dpr[:, h0 : h0 + blk] - scale[h0][1])
            ).astype(BF16)
        pair = split // 2
        for k0 in (split + pair, pair, split, 0):
            y = mm(pt[k0 * keys : (k0 + pair) * keys, :], gall[...])
            if k0 == 0:
                own = y[:keys]
            part[k0 : k0 + pair] = y.astype(BF16).reshape(pair, keys, chan)
            for k in range(max(k0, 1), k0 + pair):
                scatters.append(remote(part.at[k], recv.at[k], at(-2 * slot_shift[k], 0)))
                scatters[-1].start()

        utb[...] = mm(ntr[...], pt[...]).astype(BF16)
        ident_g = eye(gq)
        mine = None
        for owner in (1, 0):
            outs = []
            qfeat = jnp.zeros((ps, chan), F32)
            for g in range(groups):
                for which in range(2):
                    c0 = (2 * which + owner) * hq + g * gq
                    u = mm(ident_g, utb[:, c0 : c0 + gq], NT).astype(BF16)
                    w = (wv, wk)[which][:, g * chan : (g + 1) * chan]
                    y = jnp.where(head_mask, mm(u, w), 0.0).reshape(group, ps, chan).sum(axis=0)
                    if which == 0:
                        outs.append(y)
                    else:
                        y = (y * HEAD_DIM**-0.5).astype(BF16)
                        qfeat = qfeat + mm(y, wq[:, g * chan : (g + 1) * chan], NT)
            if owner == 1:
                for g in range(groups):
                    joined[0, :, g * chan : (g + 1) * chan] = outs[g]
                joined[0, :, width : width + chan] = qfeat
                joins = remote(joined.at[0], joined.at[1], sibling)
                joins.start()
            else:
                mine = (outs, qfeat)
        joins.wait()
        outs, qfeat = mine
        for g in range(groups):
            cell = slice(g * chan, (g + 1) * chan)
            attended[0, :, cell] = (outs[g] + joined[1, :, cell]).astype(BF16)
        qfeat = qfeat + joined[1, :, width : width + chan]

        zero = jnp.zeros_like(qfeat)
        total = own + jnp.concatenate(
            [jnp.where(first, qfeat, zero), jnp.where(first, zero, qfeat)], axis=0
        )
        wait(scatters)
        wait(slope_rows + slope_cols + slope_ends)
        total = total + recv[1:].astype(F32).sum(axis=0)
        pgrad = inv_std * (
            total
            - total.mean(-1, keepdims=True)
            - standard * (total * standard).mean(-1, keepdims=True)
        )
        pgb[...] = pgrad.astype(BF16).reshape(pr, ps, chan)
        for side in range(2):
            for p in range(pr):
                r = p * ps + (ps - 1, 0)[side]
                pgcell[side * pr + p : side * pr + p + 1, :] = pgrad[r : r + 1]
        pg_rows = [
            remote(pgb.at[0], pgrow.at[1], at(0, -1)),
            remote(pgb.at[pr - 1], pgrow.at[0], at(0, 1)),
        ]
        pg_cols, pg_ends = [], []
        for side, place, dlon, dlat in halo:
            if place == 0:
                src, dst = pgcell.at[pl.ds(side * pr, pr)], pgmid.at[side, pl.ds(0, pr)]
                pg_cols.append(remote(src, dst, at(dlon, dlat)))
            else:
                src = pgcell.at[pl.ds(side * pr + (pr - 1 if place == 1 else 0), 1)]
                dst = pgend.at[side, place - 1, pl.ds(0, 1)]
                pg_ends.append(remote(src, dst, at(dlon, dlat)))
        start(pg_ends + pg_rows + pg_cols)

        cg[0] = jnp.zeros((slab_rows, chan), BF16)
        cg[rows + 1] = jnp.zeros((slab_rows, chan), BF16)
        for i in range(rows):
            p = i // POOL
            pg = pgrad[p * ps : (p + 1) * ps]
            slabs = [
                pg * dsl[i * cols + t * ps : i * cols + (t + 1) * ps, :] for t in range(POOL)
            ]
            for t, slab in enumerate(padded(slabs, 0.0, 0.0)):
                cg[1 + i, t * ps : (t + 1) * ps, :] = slab
        weights = jnp.concatenate([cw[a, b] for a in range(3) for b in range(3)], axis=1)
        y = mm(windows(cg, rows, cols, ps, True), weights, NT)
        wrow = lax.broadcasted_iota(jnp.int32, (cols, cols), 0)
        wcol = lax.broadcasted_iota(jnp.int32, (cols, cols), 1)
        weave = jnp.where(
            wrow == lax.rem(wcol, ps) * POOL + lax.div(wcol, ps), 1.0, 0.0
        ).astype(BF16)
        grow[0] = y[:cols]
        grow[1] = y[(rows - 1) * cols :]
        for i in range(1, rows - 1):
            gout[i] = mm(weave, y[i * cols : (i + 1) * cols].astype(BF16)).astype(BF16)

        wait(pg_cols)
        halves = []
        for side in range(2):
            cells = jnp.where(line < POOL, pgmid[side, 0:1, :], pgmid[side, 1:2, :])
            halves.append(column_taps(cells * colhalo[1, side])[::-1])
        fixes = column_terms(
            halves[0],
            halves[1],
            [cw[a, 2] for a in range(3)] + [cw[a, 0] for a in range(3)],
            NT,
        )
        tile_row = lax.broadcasted_iota(jnp.int32, (16, chan), 0)
        for k in range(2):
            i = k * (rows - 1)
            grow[k, 0:ps, :] = grow[k, 0:ps, :] + jnp.where(edge == 0, fixes[0][i : i + 1], 0.0)
            grow[k, cols - ps : cols, :] = grow[k, cols - ps : cols, :] + jnp.where(
                edge == ps - 1, fixes[1][i : i + 1], 0.0
            )
        for i in range(1, rows - 1):
            for side, cut, cell in ((0, slice(0, 16), 0), (1, slice(cols - 16, cols), 15)):
                gout[i, cut, :] = (
                    gout[i, cut, :].astype(F32)
                    + jnp.where(tile_row == cell, fixes[side][i : i + 1], 0.0)
                ).astype(BF16)
        wait(pg_rows + pg_ends)
        lhs = []
        for k in range(2):
            pg = pgrow[k].astype(F32)
            slope = dslhalo[k].astype(F32)
            slabs = [pg * slope[t * ps : (t + 1) * ps] for t in range(POOL)]
            slabs = padded(
                slabs,
                pgend[0, k, 0:1, :] * colend[1, 0, k, 0:1, :],
                pgend[1, k, 0:1, :] * colend[1, 1, k, 0:1, :],
            )
            lhs.append(row_windows(slabs, (2, 1, 0)))
        y = [
            mm(lhs[k], jnp.concatenate([cw[2 - 2 * k, b] for b in range(3)], axis=1), NT)
            for k in range(2)
        ]
        for k in range(2):
            out = grow[k] + y[k] * poles[k]
            gout[k * (rows - 1)] = mm(weave, out.astype(BF16)).astype(BF16)

    return kernel


def store_kernel(att, gout, attended, out_grad, sem):
    copies = [
        pltpu.make_async_copy(gout, out_grad, sem.at[0]),
        pltpu.make_async_copy(att, attended, sem.at[1]),
    ]
    for copy in copies:
        copy.start()
    for copy in copies:
        copy.wait()


def solution(mesh):
    lon_n, lat_n = mesh.shape["lon"], mesh.shape["lat"]

    def on_device(field, conv_w, wq, wk, wv, query_rows, attended_grad):
        rows, cols, chan = field.shape
        width = wq.shape[1]
        pr, ps = rows // POOL, cols // POOL
        keys = pr * ps
        chips = lon_n // 2
        hq = (width // HEAD_DIM) * ps
        slab_rows = (POOL + 2) * ps
        any_spec = pl.BlockSpec(memory_space=pl.ANY)
        vmem = pl.BlockSpec(memory_space=pltpu.VMEM)
        att, gout = pl.pallas_call(
            make_kernel(lon_n, lat_n, rows, cols, chan, width),
            out_shape=(
                pltpu.VMEM(attended_grad.shape, BF16),
                pltpu.VMEM(field.shape, BF16),
            ),
            in_specs=[any_spec] * 5 + [vmem, any_spec],
            out_specs=(vmem, vmem),
            scratch_shapes=[
                pltpu.VMEM((rows, cols, chan), BF16),
                pltpu.VMEM((rows + 2, slab_rows, chan), BF16),
                pltpu.VMEM((2, cols, chan), BF16),
                pltpu.VMEM((rows + 2, slab_rows, chan), BF16),
                pltpu.VMEM((3, 3, chan, chan), BF16),
                pltpu.VMEM((chan, width), BF16),
                pltpu.VMEM((chan, width), BF16),
                pltpu.VMEM((chan, width), BF16),
                pltpu.VMEM((2, ps, width), BF16),
                pltpu.VMEM((rows * cols, chan), F32),
                pltpu.VMEM((2, rows, chan), F32),
                pltpu.VMEM((2, cols, chan), F32),
                pltpu.VMEM((rows * cols, chan), F32),
                pltpu.VMEM((chips, keys, chan), BF16),
                pltpu.VMEM((2, ps, chan), BF16),
                pltpu.VMEM((chan, chips * keys), BF16),
                pltpu.VMEM((chips * keys, 2 * hq), F32),
                pltpu.VMEM((chips * keys, 2 * hq), F32),
                pltpu.VMEM((chips * keys, 4 * hq), BF16),
                pltpu.VMEM((chan, 4 * hq), BF16),
                pltpu.VMEM((4 * hq, chan), BF16),
                pltpu.VMEM((chips, keys, chan), BF16),
                pltpu.VMEM((chips, keys, chan), BF16),
                pltpu.VMEM((2, 8, 2 * hq), F32),
                pltpu.VMEM((2, ps, width + chan), F32),
                pltpu.VMEM((2, 2, rows, chan), F32),
                pltpu.VMEM((2, 2, rows, chan), F32),
                pltpu.VMEM((2, 2, 2, 8, chan), F32),
                pltpu.VMEM((2, cols, chan), BF16),
                pltpu.VMEM((2, cols, chan), BF16),
                pltpu.VMEM((pr, ps, chan), BF16),
                pltpu.VMEM((8, chan), F32),
                pltpu.VMEM((2, 8, chan), F32),
                pltpu.VMEM((2, 2, 8, chan), F32),
                pltpu.VMEM((2, ps, chan), BF16),
                pltpu.SemaphoreType.DMA((6,)),
                pltpu.SemaphoreType.DMA((48,)),
                pltpu.SemaphoreType.DMA((48,)),
            ],
            compiler_params=pltpu.CompilerParams(
                collective_id=0, has_side_effects=True, vmem_limit_bytes=55 * 1024 * 1024
            ),
        )(field, conv_w, wq, wk, wv, query_rows, attended_grad)
        return pl.pallas_call(
            store_kernel,
            out_shape=(
                jax.ShapeDtypeStruct(attended_grad.shape, BF16),
                jax.ShapeDtypeStruct(field.shape, BF16),
            ),
            in_specs=[vmem] * 2,
            out_specs=(any_spec, any_spec),
            scratch_shapes=[pltpu.SemaphoreType.DMA((2,))],
            compiler_params=pltpu.CompilerParams(vmem_limit_bytes=4 * 1024 * 1024),
        )(att, gout)

    return jax.shard_map(
        on_device,
        mesh=mesh,
        in_specs=(
            P("lat", "lon", None),
            P(),
            P(),
            P(),
            P(),
            P("lat", "lon", None),
            P("lat", "lon", None),
        ),
        out_specs=(P("lat", "lon", None), P("lat", "lon", None)),
        check_vma=False,
    )
```

```python
import itertools

import jax
import jax.numpy as jnp
from jax import lax
from jax.experimental import pallas as pl
from jax.experimental.pallas import tpu as pltpu
from jax.sharding import PartitionSpec as P

HEAD_DIM = 64
NORM_EPS = 1e-05
POOL = 4
BF16 = jnp.bfloat16
F32 = jnp.float32
MESH = pl.DeviceIdType.MESH

NN = (((1,), (0,)), ((), ()))
NT = (((1,), (1,)), ((), ()))


def mm(a, b, dims=NN):
    return lax.dot_general(a, b, dims, preferred_element_type=F32)


def eye(n):
    rows = lax.broadcasted_iota(jnp.int32, (n, n), 0)
    cols = lax.broadcasted_iota(jnp.int32, (n, n), 1)
    return jnp.where(rows == cols, 1.0, 0.0).astype(BF16)


def windows(ref, rows, cols, ps, flip):
    chan = ref.shape[-1]
    taps = []
    for a in range(3):
        for b in range(3):
            da, db = (2 - a, 2 - b) if flip else (a, b)
            taps.append(
                ref[da : da + rows, db * ps : db * ps + cols, :].reshape(rows * cols, chan)
            )
    return jnp.concatenate(taps, axis=1)


def silu(v):
    return v * (0.5 * jnp.tanh(0.5 * v) + 0.5)


def make_kernel(lon_n, lat_n, rows, cols, chan, width):
    pr, ps = rows // POOL, cols // POOL
    keys = pr * ps
    heads = width // HEAD_DIM
    hq = heads * ps
    group = chan // HEAD_DIM
    groups = heads // group
    gq = group * ps
    slab_rows = (POOL + 2) * ps
    chips = lon_n // 2
    slot_shift = sorted(range(chips), key=lambda e: (e % 2, min(e, chips - e)))
    split = chips // 2
    halo = [
        (0, 0, 1, 0), (1, 0, -1, 0),
        (0, 1, 1, 1), (1, 1, -1, 1),
        (0, 2, 1, -1), (1, 2, -1, -1),
    ]

    def kernel(
        field, conv_w, wq_h, wk_h, wv_h, qrow, ag_h,
        attended, gout,
        xr, xs, xh, cg, cw, wq, wk, wv, ag,
        cout, ccol, grow, dsl, nall, chosen, ntr, ex, dpr, pt, utb, gall, part, recv,
        stat, joined, colmsg, colhalo, colend, dslrow, dslhalo, pgb, pgcell, pgmid, pgend, pgrow,
        load_sem, send_sem, recv_sem,
    ):
        lon = lax.axis_index("lon")
        lat = lax.axis_index("lat")
        count = itertools.count()

        def at(dlon, dlat):
            return {
                "lon": lax.rem(lon + dlon + lon_n, lon_n),
                "lat": lax.rem(lat + dlat + lat_n, lat_n),
            }

        sibling = {"lon": lon + 1 - 2 * lax.rem(lon, 2), "lat": lat}

        def remote(src, dst, device):
            k = next(count)
            return pltpu.make_async_remote_copy(
                src_ref=src,
                dst_ref=dst,
                send_sem=send_sem.at[k],
                recv_sem=recv_sem.at[k],
                device_id=device,
                device_id_type=MESH,
            )

        def start(copies):
            for c in copies:
                c.start()

        def wait(copies):
            for c in copies:
                c.wait()

        loads = [
            pltpu.make_async_copy(field, xr, load_sem.at[0]),
            pltpu.make_async_copy(conv_w, cw, load_sem.at[1]),
            pltpu.make_async_copy(ag_h.at[0], ag.at[0], load_sem.at[2]),
            pltpu.make_async_copy(wv_h, wv, load_sem.at[3]),
            pltpu.make_async_copy(wq_h, wq, load_sem.at[4]),
            pltpu.make_async_copy(wk_h, wk, load_sem.at[5]),
        ]
        loads[0].start()

        barrier = pltpu.get_barrier_semaphore()
        friends = [(0, -1), (0, 1)] + [(dlon, dlat) for _, _, dlon, dlat in halo]
        friends += [(2 * e, 0) for e in range(1, chips)]
        for dlon, dlat in friends:
            pl.semaphore_signal(barrier, inc=1, device_id=at(dlon, dlat), device_id_type=MESH)
        start(loads[1:])

        def columns(phase):
            mids, ends = [], []
            for side, place, dlon, dlat in halo:
                if place == 0:
                    src, dst = colmsg.at[phase, side], colhalo.at[phase, side]
                    mids.append(remote(src, dst, at(dlon, dlat)))
                else:
                    cell = pl.ds(rows - 1 if place == 1 else 0, 1)
                    src = colmsg.at[phase, side, cell]
                    dst = colend.at[phase, side, place - 1, pl.ds(0, 1)]
                    ends.append(remote(src, dst, at(dlon, dlat)))
            return mids, ends

        prow = lax.broadcasted_iota(jnp.int32, (slab_rows, cols), 0)
        pcol = lax.broadcasted_iota(jnp.int32, (slab_rows, cols), 1)
        spread = jnp.where(
            pcol == lax.rem(prow, ps) * POOL + lax.div(prow, ps) - 1, 1.0, 0.0
        ).astype(BF16)
        mid = pl.ds(ps, cols)

        loads[0].wait()
        for i in (0, rows - 1):
            xs[1 + i] = mm(spread, xr[i]).astype(BF16)
        for i in range(rows):
            colmsg[0, 0, i : i + 1, :] = xr[i, cols - 16 : cols, :].astype(F32)[15:16]
            colmsg[0, 1, i : i + 1, :] = xr[i, 0:16, :].astype(F32)[0:1]
        pl.semaphore_wait(barrier, len(friends))
        field_rows = [
            remote(xs.at[1, mid], xh.at[1], at(0, -1)),
            remote(xs.at[rows, mid], xh.at[0], at(0, 1)),
        ]
        field_cols, field_ends = columns(0)
        grads = remote(ag_h.at[0], ag.at[1], sibling)
        start(field_ends + field_rows + field_cols)

        xs[0] = jnp.zeros((slab_rows, chan), BF16)
        xs[rows + 1] = jnp.zeros((slab_rows, chan), BF16)
        for i in range(1, rows - 1):
            xs[1 + i] = mm(spread, xr[i]).astype(BF16)
        loads[1].wait()
        cout[...] = mm(windows(xs, rows, cols, ps, False), cw[...].reshape(9 * chan, chan))
        pooled = []
        for p in range(pr):
            lo, hi = max(p * POOL, 1), min((p + 1) * POOL, rows - 1)
            act = silu(cout[lo * cols : hi * cols, :])
            pooled.append(act.reshape((hi - lo) * POOL, ps, chan).sum(axis=0))
        for i in range(rows):
            ccol[0, i : i + 1, :] = cout[i * cols : i * cols + 1, :]
            ccol[1, i : i + 1, :] = cout[(i + 1) * cols - 1 : (i + 1) * cols, :]

        edge = lax.broadcasted_iota(jnp.int32, (ps, chan), 0)
        line = lax.broadcasted_iota(jnp.int32, (rows, chan), 0)

        def column_taps(cells):
            above = jnp.where(line == 0, 0.0, pltpu.roll(cells, 1, 0))
            below = jnp.where(line == rows - 1, 0.0, pltpu.roll(cells, rows - 1, 0))
            return above, cells, below

        def column_terms(left, right, weights, dims):
            none = jnp.zeros((rows, 3 * chan), F32)
            left, right = jnp.concatenate(left, axis=1), jnp.concatenate(right, axis=1)
            lhs = jnp.concatenate(
                [
                    jnp.concatenate([left, none], axis=1),
                    jnp.concatenate([none, right], axis=1),
                ],
                axis=0,
            ).astype(BF16)
            axis = 1 if dims == NT else 0
            y = mm(lhs, jnp.concatenate(weights, axis=axis), dims)
            return y[:rows], y[rows:]

        def padded(slabs, left, right):
            lo = jnp.where(edge == 0, left, pltpu.roll(slabs[POOL - 1], 1, 0))
            hi = jnp.where(edge == ps - 1, right, pltpu.roll(slabs[0], ps - 1, 0))
            return [slab.astype(BF16) for slab in [lo, *slabs, hi]]

        def row_windows(slabs, shifts):
            return jnp.concatenate(
                [jnp.concatenate(slabs[b : b + POOL], axis=0) for b in shifts], axis=1
            )

        hrow = lax.div(lax.broadcasted_iota(jnp.int32, (gq, chan), 0), ps)
        hcol = lax.div(lax.broadcasted_iota(jnp.int32, (gq, chan), 1), HEAD_DIM)
        head_mask = hrow == hcol

        def absorb(x, w_ref, base, scale):
            for g in range(groups):
                x_g = x[:, g * chan : (g + 1) * chan]
                wide = jnp.where(head_mask, jnp.concatenate([x_g] * group, axis=0), 0.0)
                y = mm(wide.astype(BF16), w_ref[:, g * chan : (g + 1) * chan], NT)
                y = y * scale if scale != 1.0 else y
                gall[base + g * gq : base + (g + 1) * gq, :] = y.astype(BF16)

        loads[2].wait()
        loads[3].wait()
        absorb(ag[0].astype(F32), wv, 0, 1.0)

        wait(field_cols)
        fixes = column_terms(
            column_taps(colhalo[0, 0]),
            column_taps(colhalo[0, 1]),
            [cw[a, 0] for a in range(3)] + [cw[a, 2] for a in range(3)],
            NN,
        )
        for side in range(2):
            before = ccol[side]
            after = before + fixes[side]
            ccol[side] = after
            change = silu(after) - silu(before)
            cell = edge == (0, ps - 1)[side]
            for p in range(pr):
                lo, hi = max(p * POOL, 1), min((p + 1) * POOL, rows - 1)
                part_sum = jnp.where((line >= lo) & (line < hi), change, 0.0).sum(
                    axis=0, keepdims=True
                )
                pooled[p] = pooled[p] + jnp.where(cell, part_sum, 0.0)
        for i in range(rows):
            cout[i * cols : i * cols + 1, :] = ccol[0, i : i + 1, :]
            cout[(i + 1) * cols - 1 : (i + 1) * cols, :] = ccol[1, i : i + 1, :]
        grads.start()
        wait(field_rows + field_ends)
        poles = [jnp.where(lat == pole, 0.0, 1.0) for pole in (0, lat_n - 1)]
        lhs = []
        for k in range(2):
            slabs = [xh[k, t * ps : (t + 1) * ps, :].astype(F32) for t in range(POOL)]
            slabs = padded(slabs, colend[0, 0, k, 0:1, :], colend[0, 1, k, 0:1, :])
            lhs.append(row_windows(slabs, range(3)))
        fix = [mm(lhs[k], cw[2 * k].reshape(3 * chan, chan)) * poles[k] for k in range(2)]
        for k in range(2):
            i = k * (rows - 1)
            v = cout[i * cols : (i + 1) * cols, :] + fix[k]
            cout[i * cols : (i + 1) * cols, :] = v
            p = k * (pr - 1)
            pooled[p] = pooled[p] + silu(v).reshape(POOL, ps, chan).sum(axis=0)
        pooled = jnp.concatenate(pooled, axis=0) * (1.0 / (POOL * POOL))
        centred = pooled - pooled.mean(-1, keepdims=True)
        inv_std = lax.rsqrt((centred * centred).mean(-1, keepdims=True) + NORM_EPS)
        standard = centred * inv_std
        nall[0] = standard.astype(BF16)
        first = qrow[0] == 0
        chosen[0] = jnp.where(first, standard[:ps], standard[ps:]).astype(BF16)

        gathers = [
            remote(nall.at[0], nall.at[k], at(2 * slot_shift[k], 0)) for k in range(1, chips)
        ]
        picks = remote(chosen.at[0], chosen.at[1], sibling)
        start([picks] + gathers[: split - 2 : -1] + gathers[split - 2 :: -1])

        loads[4].wait()
        loads[5].wait()
        picks.wait()
        q = mm(chosen[...].reshape(2 * ps, chan), wq[...]).astype(BF16).astype(F32)
        absorb(q[:ps], wk, 2 * hq, HEAD_DIM**-0.5)
        absorb(q[ps:], wk, 3 * hq, HEAD_DIM**-0.5)
        grads.wait()
        absorb(ag[1].astype(F32), wv, hq, 1.0)
        for i in range(rows):
            v = cout[i * cols : (i + 1) * cols, :]
            sig = 0.5 * jnp.tanh(0.5 * v) + 0.5
            d = sig * (1.0 + v * (1.0 - sig)) * (1.0 / (POOL * POOL))
            dsl[i * cols : (i + 1) * cols, :] = d
            colmsg[1, 1, i : i + 1, :] = d[0:1]
            colmsg[1, 0, i : i + 1, :] = d[cols - 1 : cols]
            if i == 0:
                dslrow[0] = d.astype(BF16)
            if i == rows - 1:
                dslrow[1] = d.astype(BF16)
        ident = eye(chan)

        wait(gathers)
        slope_rows = [
            remote(dslrow.at[0], dslhalo.at[1], at(0, -1)),
            remote(dslrow.at[1], dslhalo.at[0], at(0, 1)),
        ]
        slope_cols, slope_ends = columns(1)
        start(slope_rows + slope_cols + slope_ends)
        blk = 2 * chan
        nv = nall[...].reshape(chips * keys, chan)
        for h0 in range(0, 2 * hq, blk):
            s = mm(nv, gall[2 * hq + h0 : 2 * hq + h0 + blk, :], NT)
            top = s.max(axis=0, keepdims=True)
            e = jnp.exp(s - top)
            dp = mm(nv, gall[h0 : h0 + blk, :], NT)
            ex[:, h0 : h0 + blk] = e
            dpr[:, h0 : h0 + blk] = dp
            stat[0, 0:1, h0 : h0 + blk] = top
            stat[0, 1:2, h0 : h0 + blk] = e.sum(axis=0, keepdims=True)
            stat[0, 2:3, h0 : h0 + blk] = (e * dp).sum(axis=0, keepdims=True)
        stats = remote(stat.at[0], stat.at[1], sibling)
        stats.start()
        ntr[...] = mm(ident, nv, NT).astype(BF16)
        stats.wait()
        scale = {}
        for h0 in range(0, 2 * hq, blk):
            o0 = (h0 + hq) % (2 * hq)
            top, size, dot = (stat[0, k : k + 1, h0 : h0 + blk] for k in range(3))
            top2, size2, dot2 = (stat[1, k : k + 1, o0 : o0 + blk] for k in range(3))
            peak = jnp.maximum(top, top2)
            f, f2 = jnp.exp(top - peak), jnp.exp(top2 - peak)
            inv = 1.0 / (size * f + size2 * f2)
            scale[h0] = (f * inv, (dot * f + dot2 * f2) * inv)

        scatters = []
        own = None
        for h0 in range(0, 2 * hq, blk):
            prob = ex[:, h0 : h0 + blk] * scale[h0][0]
            pt[:, h0 : h0 + blk] = prob.astype(BF16)
            pt[:, 2 * hq + h0 : 2 * hq + h0 + blk] = (
                prob * (dpr[:, h0 : h0 + blk] - scale[h0][1])
            ).astype(BF16)
        for k0 in (split, 0):
            y = mm(pt[k0 * keys : (k0 + split) * keys, :], gall[...])
            if k0 == 0:
                own = y[:keys]
            part[k0 : k0 + split] = y.astype(BF16).reshape(split, keys, chan)
            for k in range(k0 + split - 1, max(k0, 1) - 1, -1):
                scatters.append(remote(part.at[k], recv.at[k], at(-2 * slot_shift[k], 0)))
                scatters[-1].start()

        utb[...] = mm(ntr[...], pt[...]).astype(BF16)
        ident_g = eye(gq)
        mine = None
        for owner in (1, 0):
            outs = []
            qfeat = jnp.zeros((ps, chan), F32)
            for g in range(groups):
                for which in range(2):
                    c0 = (2 * which + owner) * hq + g * gq
                    u = mm(ident_g, utb[:, c0 : c0 + gq], NT).astype(BF16)
                    w = (wv, wk)[which][:, g * chan : (g + 1) * chan]
                    y = jnp.where(head_mask, mm(u, w), 0.0).reshape(group, ps, chan).sum(axis=0)
                    if which == 0:
                        outs.append(y)
                    else:
                        y = (y * HEAD_DIM**-0.5).astype(BF16)
                        qfeat = qfeat + mm(y, wq[:, g * chan : (g + 1) * chan], NT)
            if owner == 1:
                for g in range(groups):
                    joined[0, :, g * chan : (g + 1) * chan] = outs[g]
                joined[0, :, width : width + chan] = qfeat
                joins = remote(joined.at[0], joined.at[1], sibling)
                joins.start()
            else:
                mine = (outs, qfeat)
        joins.wait()
        outs, qfeat = mine
        for g in range(groups):
            cell = slice(g * chan, (g + 1) * chan)
            attended[0, :, cell] = (outs[g] + joined[1, :, cell]).astype(BF16)
        qfeat = qfeat + joined[1, :, width : width + chan]

        zero = jnp.zeros_like(qfeat)
        total = own + jnp.concatenate(
            [jnp.where(first, qfeat, zero), jnp.where(first, zero, qfeat)], axis=0
        )
        wait(scatters)
        wait(slope_rows + slope_cols + slope_ends)
        total = total + recv[1:].astype(F32).sum(axis=0)
        pgrad = inv_std * (
            total
            - total.mean(-1, keepdims=True)
            - standard * (total * standard).mean(-1, keepdims=True)
        )
        pgb[...] = pgrad.astype(BF16).reshape(pr, ps, chan)
        for side in range(2):
            for p in range(pr):
                r = p * ps + (ps - 1, 0)[side]
                pgcell[side * pr + p : side * pr + p + 1, :] = pgrad[r : r + 1]
        pg_rows = [
            remote(pgb.at[0], pgrow.at[1], at(0, -1)),
            remote(pgb.at[pr - 1], pgrow.at[0], at(0, 1)),
        ]
        pg_cols, pg_ends = [], []
        for side, place, dlon, dlat in halo:
            if place == 0:
                src, dst = pgcell.at[pl.ds(side * pr, pr)], pgmid.at[side, pl.ds(0, pr)]
                pg_cols.append(remote(src, dst, at(dlon, dlat)))
            else:
                src = pgcell.at[pl.ds(side * pr + (pr - 1 if place == 1 else 0), 1)]
                dst = pgend.at[side, place - 1, pl.ds(0, 1)]
                pg_ends.append(remote(src, dst, at(dlon, dlat)))
        start(pg_ends + pg_rows + pg_cols)

        cg[0] = jnp.zeros((slab_rows, chan), BF16)
        cg[rows + 1] = jnp.zeros((slab_rows, chan), BF16)
        for i in range(rows):
            p = i // POOL
            pg = pgrad[p * ps : (p + 1) * ps]
            slabs = [
                pg * dsl[i * cols + t * ps : i * cols + (t + 1) * ps, :] for t in range(POOL)
            ]
            for t, slab in enumerate(padded(slabs, 0.0, 0.0)):
                cg[1 + i, t * ps : (t + 1) * ps, :] = slab
        weights = jnp.concatenate([cw[a, b] for a in range(3) for b in range(3)], axis=1)
        y = mm(windows(cg, rows, cols, ps, True), weights, NT)
        wrow = lax.broadcasted_iota(jnp.int32, (cols, cols), 0)
        wcol = lax.broadcasted_iota(jnp.int32, (cols, cols), 1)
        weave = jnp.where(
            wrow == lax.rem(wcol, ps) * POOL + lax.div(wcol, ps), 1.0, 0.0
        ).astype(BF16)
        grow[0] = y[:cols]
        grow[1] = y[(rows - 1) * cols :]
        for i in range(1, rows - 1):
            gout[i] = mm(weave, y[i * cols : (i + 1) * cols].astype(BF16)).astype(BF16)

        wait(pg_cols)
        halves = []
        for side in range(2):
            cells = jnp.where(line < POOL, pgmid[side, 0:1, :], pgmid[side, 1:2, :])
            halves.append(column_taps(cells * colhalo[1, side])[::-1])
        fixes = column_terms(
            halves[0],
            halves[1],
            [cw[a, 2] for a in range(3)] + [cw[a, 0] for a in range(3)],
            NT,
        )
        tile_row = lax.broadcasted_iota(jnp.int32, (16, chan), 0)
        for k in range(2):
            i = k * (rows - 1)
            grow[k, 0:ps, :] = grow[k, 0:ps, :] + jnp.where(edge == 0, fixes[0][i : i + 1], 0.0)
            grow[k, cols - ps : cols, :] = grow[k, cols - ps : cols, :] + jnp.where(
                edge == ps - 1, fixes[1][i : i + 1], 0.0
            )
        for i in range(1, rows - 1):
            for side, cut, cell in ((0, slice(0, 16), 0), (1, slice(cols - 16, cols), 15)):
                gout[i, cut, :] = (
                    gout[i, cut, :].astype(F32)
                    + jnp.where(tile_row == cell, fixes[side][i : i + 1], 0.0)
                ).astype(BF16)
        wait(pg_rows + pg_ends)
        lhs = []
        for k in range(2):
            pg = pgrow[k].astype(F32)
            slope = dslhalo[k].astype(F32)
            slabs = [pg * slope[t * ps : (t + 1) * ps] for t in range(POOL)]
            slabs = padded(
                slabs,
                pgend[0, k, 0:1, :] * colend[1, 0, k, 0:1, :],
                pgend[1, k, 0:1, :] * colend[1, 1, k, 0:1, :],
            )
            lhs.append(row_windows(slabs, (2, 1, 0)))
        y = [
            mm(lhs[k], jnp.concatenate([cw[2 - 2 * k, b] for b in range(3)], axis=1), NT)
            for k in range(2)
        ]
        for k in range(2):
            out = grow[k] + y[k] * poles[k]
            gout[k * (rows - 1)] = mm(weave, out.astype(BF16)).astype(BF16)

    return kernel


def store_kernel(att, gout, attended, out_grad, sem):
    copies = [
        pltpu.make_async_copy(gout, out_grad, sem.at[0]),
        pltpu.make_async_copy(att, attended, sem.at[1]),
    ]
    for copy in copies:
        copy.start()
    for copy in copies:
        copy.wait()


def solution(mesh):
    lon_n, lat_n = mesh.shape["lon"], mesh.shape["lat"]

    def on_device(field, conv_w, wq, wk, wv, query_rows, attended_grad):
        rows, cols, chan = field.shape
        width = wq.shape[1]
        pr, ps = rows // POOL, cols // POOL
        keys = pr * ps
        chips = lon_n // 2
        hq = (width // HEAD_DIM) * ps
        slab_rows = (POOL + 2) * ps
        any_spec = pl.BlockSpec(memory_space=pl.ANY)
        vmem = pl.BlockSpec(memory_space=pltpu.VMEM)
        att, gout = pl.pallas_call(
            make_kernel(lon_n, lat_n, rows, cols, chan, width),
            out_shape=(
                pltpu.VMEM(attended_grad.shape, BF16),
                pltpu.VMEM(field.shape, BF16),
            ),
            in_specs=[any_spec] * 5 + [vmem, any_spec],
            out_specs=(vmem, vmem),
            scratch_shapes=[
                pltpu.VMEM((rows, cols, chan), BF16),
                pltpu.VMEM((rows + 2, slab_rows, chan), BF16),
                pltpu.VMEM((2, cols, chan), BF16),
                pltpu.VMEM((rows + 2, slab_rows, chan), BF16),
                pltpu.VMEM((3, 3, chan, chan), BF16),
                pltpu.VMEM((chan, width), BF16),
                pltpu.VMEM((chan, width), BF16),
                pltpu.VMEM((chan, width), BF16),
                pltpu.VMEM((2, ps, width), BF16),
                pltpu.VMEM((rows * cols, chan), F32),
                pltpu.VMEM((2, rows, chan), F32),
                pltpu.VMEM((2, cols, chan), F32),
                pltpu.VMEM((rows * cols, chan), F32),
                pltpu.VMEM((chips, keys, chan), BF16),
                pltpu.VMEM((2, ps, chan), BF16),
                pltpu.VMEM((chan, chips * keys), BF16),
                pltpu.VMEM((chips * keys, 2 * hq), F32),
                pltpu.VMEM((chips * keys, 2 * hq), F32),
                pltpu.VMEM((chips * keys, 4 * hq), BF16),
                pltpu.VMEM((chan, 4 * hq), BF16),
                pltpu.VMEM((4 * hq, chan), BF16),
                pltpu.VMEM((chips, keys, chan), BF16),
                pltpu.VMEM((chips, keys, chan), BF16),
                pltpu.VMEM((2, 8, 2 * hq), F32),
                pltpu.VMEM((2, ps, width + chan), F32),
                pltpu.VMEM((2, 2, rows, chan), F32),
                pltpu.VMEM((2, 2, rows, chan), F32),
                pltpu.VMEM((2, 2, 2, 8, chan), F32),
                pltpu.VMEM((2, cols, chan), BF16),
                pltpu.VMEM((2, cols, chan), BF16),
                pltpu.VMEM((pr, ps, chan), BF16),
                pltpu.VMEM((8, chan), F32),
                pltpu.VMEM((2, 8, chan), F32),
                pltpu.VMEM((2, 2, 8, chan), F32),
                pltpu.VMEM((2, ps, chan), BF16),
                pltpu.SemaphoreType.DMA((6,)),
                pltpu.SemaphoreType.DMA((48,)),
                pltpu.SemaphoreType.DMA((48,)),
            ],
            compiler_params=pltpu.CompilerParams(
                collective_id=0, has_side_effects=True, vmem_limit_bytes=55 * 1024 * 1024
            ),
        )(field, conv_w, wq, wk, wv, query_rows, attended_grad)
        return pl.pallas_call(
            store_kernel,
            out_shape=(
                jax.ShapeDtypeStruct(attended_grad.shape, BF16),
                jax.ShapeDtypeStruct(field.shape, BF16),
            ),
            in_specs=[vmem] * 2,
            out_specs=(any_spec, any_spec),
            scratch_shapes=[pltpu.SemaphoreType.DMA((2,))],
            compiler_params=pltpu.CompilerParams(vmem_limit_bytes=4 * 1024 * 1024),
        )(att, gout)

    return jax.shard_map(
        on_device,
        mesh=mesh,
        in_specs=(
            P("lat", "lon", None),
            P(),
            P(),
            P(),
            P(),
            P("lat", "lon", None),
            P("lat", "lon", None),
        ),
        out_specs=(P("lat", "lon", None), P("lat", "lon", None)),
        check_vma=False,
    )
```
